512 devices in a mesh: dom: 128 (over y, z, core), type: 4 (over x).
Axes of the slice: x: 4, y: 8, z: 8, core: 2. Of those that a mesh axis runs over, the one named last changes fastest.
Arguments:
- vertex_table: bfloat16 [262144, 128], P(('dom', 'type')), may hold values from -3 to 3
- context_table: bfloat16 [262144, 128], P(('dom', 'type')), may hold values from -3 to 3
- vertex_state: float32 [262144], P(('dom', 'type')), may hold values from 0.05 to 2
- context_state: float32 [262144], P(('dom', 'type')), may hold values from 0.05 to 2
- pair_blocks: int32 [2, 4096, 2], P(None, ('dom', 'type')), may hold values from 0 to 3
- pair_offsets: int32 [2, 4096, 16, 2], P(None, ('dom', 'type')), may hold values from 0 to 127
- negative_owner: int32 [2, 4096, 16, 5], P(None, ('dom', 'type')), may hold values from 0 to 511, all different within a row; in each aligned block of 128 rows (0 to 127, 128 to 255, ..., all dimensions but the last counted through in order) at most 3 rows name the same one
- negative_row: int32 [2, 4096, 16, 5], P(None, ('dom', 'type')), may hold values from 0 to 511
Outputs:
- new_vertex: bfloat16 [262144, 128], P(('dom', 'type'))
- new_context: bfloat16 [262144, 128], P(('dom', 'type'))
- new_vertex_state: float32 [262144], P(('dom', 'type'))
- new_context_state: float32 [262144], P(('dom', 'type'))
The draws below stay inside these ranges and needn't reach their ends.
Inputs may be any that keep to these rules, and one draw needn't show every extreme that they name: `negative_owner`: in each episode, among the 5 negatives of all 128 pairs of one device, no owner is named more than 3 times, a bound that some block reaches; the 5 owners of one pair differ.
All inputs are finite; a program needn't handle non-finite values.
Results may differ from the reference program's by a relative error of at most 0.009.
Values may be sent and summed in bfloat16 or wider, within the bound.
No kernel may reach another device: no remote copies, remote signals or barrier semaphores. Data moves between devices by JAX's collectives and lax.ppermute only.
A program may use at most 64 MiB of HBM per device.

```python
import math
import jax
import jax.numpy as jnp
import numpy as np
from jax import lax

D = 128
TILE = 128
ROWS = 512
BP = 8
PPB = 16
NEG = 5
EPIS = 2
BP_ALL = 4096
NODES = 262144
CAP = 3
N_DOM = 128
N_TYPE = 4
DEVICES = 512


def set_ends(drawn, stream_key, low, high):
    spot = [jax.random.randint(jax.random.fold_in(stream_key, axis), (), 0, length) for axis, length in enumerate(drawn.shape)]
    widest = drawn.shape.index(max(drawn.shape))
    neighbour = spot[:widest] + [(spot[widest] + 1) % drawn.shape[widest]] + spot[widest + 1:]
    return drawn.at[tuple(spot)].set(low).at[tuple(neighbour)].set(high)


def shard_levels(stream_key, shape, split, low, high):
    factor_of = 1.0
    for dim, blocks in split:
        draws = jax.random.uniform(jax.random.fold_in(jax.random.fold_in(stream_key, 6), dim), (blocks,), jnp.float32, low / len(split), high / len(split))
        factor_of = factor_of * jnp.repeat(jnp.exp(draws), shape[dim] // blocks).reshape((-1,) + (1,) * (len(shape) - 1 - dim))
    return factor_of


def deal_out(own_key, own, number, rows, number_of, top, limit, skew):
    order = jax.random.permutation(own_key, number_of)
    heavy_load, usual = load_shares(number_of, rows * top, limit, skew, True), load_shares(number_of, rows * top, limit, skew, False)
    places = jnp.arange(number_of)

    def named(sizes, rotation):
        used = int((sizes > 0).sum())
        fixed = max(1, used // 4)
        passed = fixed + (places - fixed + rotation * (used - fixed)) % max(1, number_of - fixed)
        return jnp.zeros((number_of,), jnp.int32).at[order[jnp.where(places < fixed, places, passed)]].set(jnp.asarray(sizes, jnp.int32))

    sizes = jnp.where(number % 4 == 0, named(heavy_load, number // 4), named(usual, number - number // 4 - 1))
    mixed = jax.random.permutation(jax.random.fold_in(own, 3), number_of)
    donor, receiver = mixed[0:number_of // 2 * 2:2], mixed[1:number_of // 2 * 2:2]
    margin = jnp.minimum(sizes[donor] - 1, limit - sizes[receiver]) // 2
    margin = jnp.where((donor == order[0]) | (receiver == order[0]) | (sizes[receiver] == 0), 0, jnp.maximum(margin, 0))
    passed = jax.random.randint(jax.random.fold_in(own, 4), (number_of // 2,), 0, 1 << 20) % (margin + 1)
    sizes = sizes.at[donor].add(-passed).at[receiver].add(passed)
    members = jnp.searchsorted(jnp.cumsum(sizes), jnp.arange(rows * top), side="right").astype(jnp.int32)
    grid = members.reshape(top, rows).T
    grid = grid[jax.random.permutation(jax.random.fold_in(own, 1), rows)]
    rotation = jax.random.randint(jax.random.fold_in(own, 2), (rows, 1), 0, top)
    return jnp.take_along_axis(grid, (jnp.arange(top)[None, :] + rotation) % top, axis=1)


def load_shares(number_of, total, limit, skew, full):
    weights = [(1 << 20) // math.isqrt(standing ** skew) + 1 for standing in range(1, number_of + 1)]
    largest = limit if full else min(limit, max(-(-total // number_of), total * weights[0] // sum(weights)))
    least = 1 if total - largest >= number_of - 1 else 0
    holding, spare = [largest] + [least] * (number_of - 1), total - largest - least * (number_of - 1)
    while spare > 0:
        movable = [i for i in range(1, number_of) if holding[i] < largest] or [i for i in range(1, number_of) if holding[i] < limit]
        pool, remaining = sum([weights[i] for i in movable]), spare
        for i in movable:
            extra = min(limit - holding[i], max(1, remaining * weights[i] // pool), spare)
            holding[i] = holding[i] + extra
            spare = spare - extra
    return np.array(holding)


def noise(rng, extent, scale, bound, split=(), held_as=jnp.bfloat16):
    result = jax.random.normal(rng, extent, jnp.float32) * scale
    if len(split) > 0:
        result = shard_levels(rng, extent, split, -0.22, 0.18) * result
    return jnp.clip(result, min=-bound, max=bound).astype(held_as)


def setup_inputs(seed: int = 0) -> dict:
    seeds = jax.random.split(jax.random.key(seed), 9)
    vertex_table = noise(seeds[0], (NODES, D), 0.3, 3.0, ((0, 512),))
    context_table = noise(seeds[1], (NODES, D), 0.3, 3.0, ((0, 512),))
    vertex_state = jnp.clip(jnp.exp(math.log(2.0) - 3.6888794 * jax.random.uniform(seeds[2], (NODES,), jnp.float32) ** shard_levels(seeds[2], (NODES,), ((0, 512),), -0.2, 0.2)), 0.05, 2.0)
    context_state = jnp.clip(jnp.exp(math.log(2.0) - 3.6888794 * jax.random.uniform(seeds[3], (NODES,), jnp.float32) ** shard_levels(seeds[3], (NODES,), ((0, 512),), -0.2, 0.2)), 0.05, 2.0)
    pair_blocks = set_ends(jax.random.randint(seeds[4], (EPIS, BP_ALL, 2), 0, ROWS // TILE), jax.random.fold_in(seeds[4], 1), 0, (ROWS // TILE) - 1).astype(jnp.int32)
    pair_offsets = set_ends(jax.random.randint(seeds[5], (EPIS, BP_ALL, PPB, 2), 0, TILE), jax.random.fold_in(seeds[5], 1), 0, TILE - 1).astype(jnp.int32)
    negative_owner_keys = jax.random.split(jax.random.fold_in(seeds[6], 1), EPIS * BP_ALL * PPB // (BP * PPB))
    negative_owner_turns = jax.random.permutation(jax.random.fold_in(seeds[6], 3), EPIS * BP_ALL * PPB // (BP * PPB))
    negative_owner = jax.vmap(lambda own, number: deal_out(jax.random.fold_in(seeds[6], 2), own, number, BP * PPB, DEVICES, NEG, CAP, 1))(negative_owner_keys, negative_owner_turns).reshape((EPIS, BP_ALL, PPB, NEG))
    negative_row = set_ends(jax.random.randint(seeds[7], (EPIS, BP_ALL, PPB, NEG), 0, ROWS), jax.random.fold_in(seeds[7], 1), 0, ROWS - 1).astype(jnp.int32)
    return dict(vertex_table=vertex_table, context_table=context_table, vertex_state=vertex_state, context_state=context_state, pair_blocks=pair_blocks, pair_offsets=pair_offsets, negative_owner=negative_owner, negative_row=negative_row)


def adagrad_step(table_rows, row_state, gradient):
    new_state = row_state + lax.optimization_barrier(jnp.mean(gradient * gradient, axis=-1))
    updated = table_rows.astype(jnp.float32) - 0.5 * gradient / jnp.sqrt(new_state)[:, None]
    return (updated.astype(jnp.bfloat16), new_state)

def reference(vertex_table, context_table, vertex_state, context_state, pair_blocks, pair_offsets, negative_owner, negative_row):
    n_devices = N_DOM * N_TYPE
    n_pairs = BP * PPB
    device_ids = jnp.arange(n_devices, dtype=jnp.int32)
    for episode in range(EPIS):
        shift_by = 1 + N_TYPE * (episode + 1)
        blocks = pair_blocks[episode].reshape(n_devices, BP, 1, 2)
        offsets = pair_offsets[episode].reshape(n_devices, BP, PPB, 2)
        local_rows = (blocks * TILE + offsets).reshape(n_devices, n_pairs, 2)
        vertex_rows = device_ids[:, None] * ROWS + local_rows[:, :, 0]
        partner = (device_ids - shift_by) % n_devices
        context_rows = partner[:, None] * ROWS + local_rows[:, :, 1]
        negative_rows = negative_owner[episode].reshape(n_devices, n_pairs, NEG) * ROWS + negative_row[episode].reshape(n_devices, n_pairs, NEG)
        vectors = vertex_table[vertex_rows].astype(jnp.float32)
        positives = context_table[context_rows].astype(jnp.float32)
        negatives = context_table[negative_rows].astype(jnp.float32)
        positive_weight = jax.nn.sigmoid(lax.optimization_barrier(jnp.sum(vectors * positives, axis=-1))) - 1.0
        negative_weight = jax.nn.sigmoid(lax.optimization_barrier(jnp.sum(vectors[:, :, None, :] * negatives, axis=-1)))
        vertex_terms = positive_weight[..., None] * positives + lax.optimization_barrier(jnp.sum(negative_weight[..., None] * negatives, axis=2))
        vertex_gradient = jnp.zeros((NODES, D), jnp.float32).at[vertex_rows.reshape(-1)].add(vertex_terms.reshape(-1, D))
        context_gradient = jnp.zeros((NODES, D), jnp.float32).at[context_rows.reshape(-1)].add((positive_weight[..., None] * vectors).reshape(-1, D))
        context_gradient = context_gradient.at[negative_rows.reshape(-1)].add((negative_weight[..., None] * vectors[:, :, None, :]).reshape(-1, D))
        vertex_table, vertex_state = adagrad_step(vertex_table, vertex_state, vertex_gradient)
        context_table, context_state = adagrad_step(context_table, context_state, context_gradient)
    return (vertex_table, context_table, vertex_state, context_state)
```

```python
import jax
import jax.numpy as jnp
from jax import lax
from jax.experimental import pallas as pl
from jax.experimental.pallas import tpu as pltpu
from jax.sharding import PartitionSpec as P

AXES = ("dom", "type")
TILE = 128
CAP = 3
LANES = 128
F32 = jnp.float32
BF16 = jnp.bfloat16


def iota(shape, dim):
    return lax.broadcasted_iota(jnp.int32, shape, dim).astype(F32)


def dot(a, b):
    return jnp.dot(a, b, preferred_element_type=F32)


def eye():
    return iota((LANES, LANES), 0) == iota((LANES, LANES), 1)


def to_row(col):
    return jnp.sum(jnp.where(eye(), col, 0.0), axis=0, keepdims=True)


def to_col(row):
    return jnp.sum(jnp.where(eye(), row, 0.0), axis=1, keepdims=True)


def one_hot_of_col(col, rows):
    return jnp.where(col == iota((col.shape[0], rows), 1), 1.0, 0.0).astype(BF16)


def one_hot_of_row(row, rows, first):
    return jnp.where(row == iota((rows, row.shape[1]), 0) + first, 1.0, 0.0).astype(BF16)


def lane_of(episode, slot, part):
    return 16 * episode + 4 * slot + part


def slot_col(table, lane):
    return table[:, lane : lane + 1] * 256.0 + table[:, lane + 1 : lane + 2] - 1.0


def slot_row(turned, lane):
    return turned[lane : lane + 1, :] * 256.0 + turned[lane + 1 : lane + 2, :] - 1.0


def row_dot(a, b):
    return jnp.sum(a * b, axis=1, keepdims=True)


def blocks(n, step):
    lax.fori_loop(0, n // TILE, lambda b, c: (step(pl.multiple_of(b * TILE, TILE), b), c)[1], 0)


def turn(slots_ref, turned_ref):
    def step(at, b):
        turned_ref[b] = jnp.transpose(slots_ref[CAP, pl.ds(at, TILE), :].astype(F32))

    blocks(slots_ref.shape[1], step)


def gather_slots(table_ref, slots_ref, out_ref, first_out, episode, part):
    def step(at, b):
        slots = slots_ref[CAP, pl.ds(at, TILE), :].astype(F32)
        for s in range(CAP):
            col = slot_col(slots, lane_of(episode, s, part))
            rows = dot(one_hot_of_col(col, table_ref.shape[0]), table_ref[...])
            out_ref[first_out + s, pl.ds(at, TILE), :] = rows.astype(BF16)

    blocks(slots_ref.shape[1], step)


def weigh_slots(here_ref, first_here, there_ref, first_there, out_ref):
    def step(at, b):
        for s in range(CAP):
            here = here_ref[first_here + s, pl.ds(at, TILE), :].astype(F32)
            there = there_ref[first_there + s, pl.ds(at, TILE), :].astype(F32)
            out_ref[s, pl.ds(at, TILE), :] = (jax.nn.sigmoid(row_dot(here, there)) * there).astype(BF16)

    blocks(out_ref.shape[1], step)


def adagrad(
    table_ref, state_ref, new_ref, new_state_ref, turned_ref, terms_ref, lane0, pair_row, pair_terms
):
    owners = terms_ref.shape[1]
    width = table_ref.shape[1]

    def step(at, b):
        first = at.astype(F32)
        grad = dot(one_hot_of_row(pair_row, TILE, first), pair_terms)
        for s in range(CAP):
            for o in range(owners // TILE):
                row = slot_row(turned_ref[o], lane0 + 4 * s)
                grad += dot(one_hot_of_row(row, TILE, first), terms_ref[s, o * TILE : (o + 1) * TILE, :])
        state = jnp.transpose(jnp.broadcast_to(state_ref[pl.ds(b, 1), :], (TILE, TILE)))
        state = state + row_dot(grad, grad) * (1.0 / width)
        rows = table_ref[pl.ds(at, TILE), :].astype(F32) - 0.5 * grad / jnp.sqrt(state)
        new_ref[pl.ds(at, TILE), :] = rows.astype(BF16)
        new_state_ref[pl.ds(b, 1), :] = jnp.transpose(state)[0:1, :]

    blocks(table_ref.shape[0], step)


def pairs_out(pairs_ref, episode, table_ref, out_ref):
    pairs = pairs_ref[episode].astype(F32)
    n = pairs.shape[0]
    rows = dot(one_hot_of_col(pairs[:, 0:1], table_ref.shape[0]), table_ref[...])
    out_ref[0:n, :] = rows.astype(BF16)
    high = jnp.floor(pairs[:, 1:2] * (1.0 / 256.0))
    low = pairs[:, 1:2] - high * 256.0
    which = iota((16, LANES), 0)
    tail = jnp.where(which == 0, to_row(high), jnp.where(which == 1, to_row(low), 0.0))
    out_ref[n : n + 16, :] = tail.astype(BF16)


def pair_terms_of(here, there):
    return ((jax.nn.sigmoid(row_dot(here, there)) - 1.0) * there).astype(BF16)


def first_kernel(owner_ref, row_ref, pairs_ref, table_ref, send_ref, pair_ref):
    episodes, pairs, negatives = owner_ref.shape
    owners = send_ref.shape[1]
    lane = lax.broadcasted_iota(jnp.int32, (pairs, LANES), 1)
    slot_of_lane = ((lane // 4) % 4).astype(F32)
    earlier = iota((pairs, pairs), 1) < iota((pairs, pairs), 0)
    owner_rows, values = [], []
    for e in range(episodes):
        vertex = pairs_ref[e].astype(F32)[:, 0:1] + 1.0
        vertex_high = jnp.floor(vertex * (1.0 / 256.0))
        cols = [owner_ref[e].astype(F32)[:, k : k + 1] for k in range(negatives)]
        rows = [to_row(c) for c in cols]
        for k in range(negatives):
            same = jnp.where((cols[k] == rows[k]) & earlier, 1.0, 0.0)
            for j in range(k):
                same += jnp.where(cols[k] == rows[j], 1.0, 0.0)
            rank = jnp.sum(same, axis=1, keepdims=True)
            target = row_ref[e].astype(F32)[:, k : k + 1] + 1.0
            target_high = jnp.floor(target * (1.0 / 256.0))
            part = lane % 4
            value = jnp.where(part == 0, target_high, target - 256.0 * target_high)
            value = jnp.where(part == 2, vertex_high, value)
            value = jnp.where(part == 3, vertex - 256.0 * vertex_high, value)
            mine = (slot_of_lane == rank) & (lane // 16 == e)
            values.append(jnp.where(mine, value, 0.0).astype(BF16))
            owner_rows.append(rows[k])

    for b in range(owners // TILE):
        total = jnp.zeros((TILE, LANES), F32)
        for row, value in zip(owner_rows, values):
            total += dot(one_hot_of_row(row, TILE, float(b * TILE)), value)
        send_ref[CAP, b * TILE : (b + 1) * TILE, :] = total.astype(BF16)
    gather_slots(table_ref, send_ref, send_ref, 0, 0, 2)
    pairs_out(pairs_ref, 0, table_ref, pair_ref)


def context_side(pair_ref, table_ref):
    n = pair_ref.shape[0] - 16
    tail = pair_ref[n : n + 16, :].astype(F32)
    row = tail[0:1, :] * 256.0 + tail[1:2, :]
    mine = dot(one_hot_of_col(to_col(row), table_ref.shape[0]), table_ref[...])
    return row, pair_terms_of(mine, pair_ref[0:n, :].astype(F32))


def vertex_side(pairs_ref, episode, table_ref, partner_ref):
    pairs = pairs_ref[episode].astype(F32)
    mine = dot(one_hot_of_col(pairs[:, 0:1], table_ref.shape[0]), table_ref[...])
    theirs = dot(one_hot_of_col(pairs[:, 1:2], partner_ref.shape[0]), partner_ref[...])
    return to_row(pairs[:, 0:1]), pair_terms_of(mine, theirs)


def context_first(got_ref, pair_ref, table_ref, state_ref, send_ref, new_ref, new_state_ref, turned_ref, terms_ref):
    turn(got_ref, turned_ref)
    gather_slots(table_ref, got_ref, send_ref, 0, 0, 0)
    weigh_slots(send_ref, 0, got_ref, 0, terms_ref)
    row, pair_terms = context_side(pair_ref, table_ref)
    adagrad(
        table_ref, state_ref, new_ref, new_state_ref, turned_ref, terms_ref, lane_of(0, 0, 0), row, pair_terms
    )
    gather_slots(new_ref, got_ref, send_ref, CAP, 1, 0)


def vertex_first(
    got_ref, sent_ref, pairs_ref, partner_ref, table_ref, state_ref,
    send_ref, pair_ref, new_ref, new_state_ref, turned_ref, terms_ref,
):
    turn(sent_ref, turned_ref)
    weigh_slots(sent_ref, 0, got_ref, 0, terms_ref)
    row, pair_terms = vertex_side(pairs_ref, 0, table_ref, partner_ref)
    adagrad(
        table_ref, state_ref, new_ref, new_state_ref, turned_ref, terms_ref, lane_of(0, 0, 2), row, pair_terms
    )
    gather_slots(new_ref, sent_ref, send_ref, 0, 1, 2)
    pairs_out(pairs_ref, 1, new_ref, pair_ref)


def vertex_last(
    got_ref, sent_ref, slots_ref, pairs_ref, partner_ref, table_ref, state_ref,
    new_ref, new_state_ref, turned_ref, terms_ref,
):
    turn(slots_ref, turned_ref)
    weigh_slots(sent_ref, 0, got_ref, CAP, terms_ref)
    row, pair_terms = vertex_side(pairs_ref, 1, table_ref, partner_ref)
    adagrad(
        table_ref, state_ref, new_ref, new_state_ref, turned_ref, terms_ref, lane_of(1, 0, 2), row, pair_terms
    )


def context_last(
    got_ref, sent_ref, slots_ref, pair_ref, table_ref, state_ref, new_ref, new_state_ref, turned_ref, terms_ref
):
    turn(slots_ref, turned_ref)
    weigh_slots(sent_ref, CAP, got_ref, 0, terms_ref)
    row, pair_terms = context_side(pair_ref, table_ref)
    adagrad(
        table_ref, state_ref, new_ref, new_state_ref, turned_ref, terms_ref, lane_of(1, 0, 0), row, pair_terms
    )


def call(kernel, name, outs, scratch, *args):
    return pl.pallas_call(
        kernel,
        name=name,
        out_shape=[jax.ShapeDtypeStruct(s, d) for s, d in outs],
        scratch_shapes=scratch,
        compiler_params=pltpu.CompilerParams(vmem_limit_bytes=16 * 1024 * 1024),
        cost_estimate=pl.CostEstimate(flops=600_000_000, bytes_accessed=4_000_000, transcendentals=2000),
    )(*args)


def exchange(rows):
    return lax.all_to_all(rows, AXES, split_axis=1, concat_axis=1, tiled=True)


def exchange_packed(rows):
    s, n, w = rows.shape
    packed = rows.reshape(2, s // 2, n, w).transpose(2, 0, 1, 3).reshape(n, 2, s // 2 * w)
    packed = lax.all_to_all(packed, AXES, split_axis=0, concat_axis=0, tiled=True)
    return packed.reshape(n, 2, s // 2, w).transpose(1, 2, 0, 3).reshape(s, n, w)


def passed_along(block, distance, n_devices):
    return lax.ppermute(block, AXES, [((i - distance) % n_devices, i) for i in range(n_devices)])


def body(
    vertex_table, context_table, vertex_state, context_state, pair_blocks, pair_offsets, negative_owner, negative_row
):
    n_type = lax.axis_size("type")
    n = lax.axis_size("dom") * n_type
    rows, width = vertex_table.shape
    episodes, block_pairs, per_block, negatives = negative_owner.shape
    n_pairs = block_pairs * per_block
    shifts = [1 + n_type * (e + 1) for e in range(episodes)]
    pairs = (pair_blocks[:, :, None, :] * TILE + pair_offsets).reshape(episodes, n_pairs, 2)
    owner = negative_owner.reshape(episodes, n_pairs, negatives)
    target = negative_row.reshape(episodes, n_pairs, negatives)
    v_state = vertex_state.reshape(rows // TILE, TILE)
    c_state = context_state.reshape(rows // TILE, TILE)

    table = ((rows, width), BF16)
    state = ((rows // TILE, TILE), F32)
    pair_rows = ((n_pairs + 16, width), BF16)
    scratch = [pltpu.VMEM((n // TILE, LANES, TILE), F32), pltpu.VMEM((CAP, n, width), BF16)]

    sent_a, pair_a = call(
        first_kernel, "slots", [((CAP + 1, n, width), BF16), pair_rows], [], owner, target, pairs, vertex_table
    )
    partner_0 = passed_along(context_table, shifts[0], n)
    got_pair_a = passed_along(pair_a, n - shifts[0], n)
    got_a = exchange(sent_a)
    sent_b, context_1, c_state_1 = call(
        context_first, "context_first", [((2 * CAP, n, width), BF16), table, state], scratch,
        got_a, got_pair_a, context_table, c_state,
    )
    partner_1 = passed_along(context_1, shifts[1], n)
    got_b = exchange_packed(sent_b)
    sent_c, pair_c, vertex_1, v_state_1 = call(
        vertex_first, "vertex_first", [((CAP, n, width), BF16), pair_rows, table, state], scratch,
        got_b, sent_a, pairs, partner_0, vertex_table, v_state,
    )
    got_pair_c = passed_along(pair_c, n - shifts[1], n)
    got_c = exchange(sent_c)
    vertex_2, v_state_2 = call(
        vertex_last, "vertex_last", [table, state], scratch,
        got_b, sent_c, sent_a, pairs, partner_1, vertex_1, v_state_1,
    )
    context_2, c_state_2 = call(
        context_last, "context_last", [table, state], scratch,
        got_c, sent_b, got_a, got_pair_c, context_1, c_state_1,
    )
    return vertex_2, context_2, v_state_2.reshape(rows), c_state_2.reshape(rows)


def solution(mesh):
    in_specs = (
        P(AXES, None),
        P(AXES, None),
        P(AXES),
        P(AXES),
        P(None, AXES, None),
        P(None, AXES, None, None),
        P(None, AXES, None, None),
        P(None, AXES, None, None),
    )
    out_specs = (P(AXES, None), P(AXES, None), P(AXES), P(AXES))
    return jax.shard_map(body, mesh=mesh, in_specs=in_specs, out_specs=out_specs, check_vma=False)
```

```python
import jax
import jax.numpy as jnp
from jax import lax
from jax.experimental import pallas as pl
from jax.experimental.pallas import tpu as pltpu
from jax.sharding import PartitionSpec as P

AXES = ("dom", "type")
TILE = 128
CAP = 3
PART = 64
BLOCK = 128
LANES = 128
F32 = jnp.float32
BF16 = jnp.bfloat16


def iota(shape, dim):
    return lax.broadcasted_iota(jnp.int32, shape, dim)


def fiota(shape, dim):
    return iota(shape, dim).astype(F32)


def ones_where(mask):
    return jnp.where(mask, 1.0, 0.0).astype(BF16)


def dot(a, b):
    return jnp.dot(a, b, preferred_element_type=F32)


def eye():
    return iota((LANES, LANES), 0) == iota((LANES, LANES), 1)


def to_row(col):
    return jnp.sum(jnp.where(eye(), col, 0.0), axis=0, keepdims=True)


def to_col(row):
    return jnp.sum(jnp.where(eye(), row, 0.0), axis=1, keepdims=True)


def one_hot_of_col(col, rows):
    return ones_where(col == fiota((col.shape[0], rows), 1))


def one_hot_of_row(row, rows, first):
    return ones_where(row == fiota((rows, row.shape[1]), 0) + first)


def lane_of(episode, slot, part):
    return 16 * episode + 4 * slot + part


def slot_col(table, lane):
    return table[:, lane : lane + 1] * 256.0 + table[:, lane + 1 : lane + 2] - 1.0


def slot_row(turned_ref, lane):
    return turned_ref[lane : lane + 1, :] * 256.0 + turned_ref[lane + 1 : lane + 2, :] - 1.0


def row_dot(a, b):
    return jnp.sum(a * b, axis=1, keepdims=True)


def blocks(n, size, step):
    if n == size:
        step(0, 0)
    else:
        lax.fori_loop(0, n // size, lambda b, c: (step(pl.multiple_of(b * size, size), b), c)[1], 0)


def by_owner(slots_ref, flat_ref, slots, group):
    j = iota((group * PART, slots * PART), 1)
    move = ones_where(iota((group * PART, slots * PART), 0) == (j % PART) * group + j // PART)

    def step(at, b):
        rows = jnp.concatenate([slots_ref[s, pl.ds(at, PART), :] for s in range(slots)], axis=0)
        flat_ref[pl.ds(pl.multiple_of(at * group, PART), group * PART), :] = dot(move, rows).astype(BF16)

    blocks(slots_ref.shape[1], PART, step)


def by_slot(flat_ref, slots_ref, slots, group):
    i = iota((slots * PART, group * PART), 0)
    move = ones_where(iota((slots * PART, group * PART), 1) == (i % PART) * group + i // PART)

    def step(at, b):
        rows = dot(move, flat_ref[pl.ds(pl.multiple_of(at * group, PART), group * PART), :]).astype(BF16)
        for s in range(slots):
            slots_ref[s, pl.ds(at, PART), :] = rows[s * PART : (s + 1) * PART, :]

    blocks(slots_ref.shape[1], PART, step)


def turn(table_ref, turned_ref):
    for o in range(0, table_ref.shape[0], TILE):
        turned_ref[:, o : o + TILE] = jnp.transpose(table_ref[o : o + TILE, :].astype(F32))


def gather_slots(table_ref, slots_ref, out_ref, first_out, episode, part, after=None):
    def step(at, b):
        slots = slots_ref[pl.ds(at, BLOCK), :].astype(F32)
        for s in range(CAP):
            col = slot_col(slots, lane_of(episode, s, part))
            rows = dot(one_hot_of_col(col, table_ref.shape[0]), table_ref[...])
            out_ref[first_out + s, pl.ds(at, BLOCK), :] = rows.astype(BF16)
            if after:
                after(s, at, rows)

    blocks(slots_ref.shape[0], BLOCK, step)


def weigh_slots(here_ref, first_here, there_ref, first_there, out_ref):
    def step(at, b):
        for s in range(CAP):
            here = here_ref[first_here + s, pl.ds(at, BLOCK), :].astype(F32)
            there = there_ref[first_there + s, pl.ds(at, BLOCK), :].astype(F32)
            out_ref[s, pl.ds(at, BLOCK), :] = (jax.nn.sigmoid(row_dot(here, there)) * there).astype(BF16)

    blocks(out_ref.shape[1], BLOCK, step)


def adagrad(
    table_ref, state_ref, new_ref, new_state_ref, turned_ref, terms_ref, lane0, pair_row, pair_terms
):
    width = table_ref.shape[1]
    index = [slot_row(turned_ref, lane0 + 4 * s) for s in range(CAP)]

    def step(at, b):
        first = jnp.asarray(at).astype(F32)
        grad = dot(one_hot_of_row(pair_row, TILE, first), pair_terms)
        for s in range(CAP):
            grad += dot(one_hot_of_row(index[s], TILE, first), terms_ref[s])
        state = jnp.transpose(jnp.broadcast_to(state_ref[pl.ds(b, 1), :], (TILE, TILE)))
        state = state + row_dot(grad, grad) * (1.0 / width)
        rows = table_ref[pl.ds(at, TILE), :].astype(F32) - 0.5 * grad / jnp.sqrt(state)
        new_ref[pl.ds(at, TILE), :] = rows.astype(BF16)
        new_state_ref[pl.ds(b, 1), :] = jnp.transpose(state)[0:1, :]

    blocks(table_ref.shape[0], TILE, step)


def pairs_out(pairs_ref, episode, table_ref, out_ref):
    pairs = pairs_ref[episode].astype(F32)
    n = pairs.shape[0]
    rows = dot(one_hot_of_col(pairs[:, 0:1], table_ref.shape[0]), table_ref[...])
    out_ref[0:n, :] = rows.astype(BF16)
    high = jnp.floor(pairs[:, 1:2] * (1.0 / 256.0))
    low = pairs[:, 1:2] - high * 256.0
    which = iota((16, LANES), 0)
    tail = jnp.where(which == 0, to_row(high), jnp.where(which == 1, to_row(low), 0.0))
    out_ref[n : n + 16, :] = tail.astype(BF16)


def pair_terms_of(here, there):
    return ((jax.nn.sigmoid(row_dot(here, there)) - 1.0) * there).astype(BF16)


def first_kernel(owner_ref, row_ref, pairs_ref, table_ref, flat_ref, rows_ref, pair_ref):
    episodes, pairs, negatives = owner_ref.shape
    owners = rows_ref.shape[1]
    lane = iota((pairs, LANES), 1)
    part = lane % 4
    slot_of_lane = ((lane // 4) % 4).astype(F32)
    earlier = iota((pairs, pairs), 1) < iota((pairs, pairs), 0)
    owner_rows, values = [], []
    for e in range(episodes):
        vertex = pairs_ref[e].astype(F32)[:, 0:1] + 1.0
        vertex_high = jnp.floor(vertex * (1.0 / 256.0))
        cols = [owner_ref[e].astype(F32)[:, k : k + 1] for k in range(negatives)]
        rows = [to_row(c) for c in cols]
        for k in range(negatives):
            same = jnp.where((cols[k] == rows[k]) & earlier, 1.0, 0.0)
            for j in range(k):
                same += jnp.where(cols[k] == rows[j], 1.0, 0.0)
            rank = jnp.sum(same, axis=1, keepdims=True)
            target = row_ref[e].astype(F32)[:, k : k + 1] + 1.0
            target_high = jnp.floor(target * (1.0 / 256.0))
            value = jnp.where(part == 0, target_high, target - 256.0 * target_high)
            value = jnp.where(part == 2, vertex_high, value)
            value = jnp.where(part == 3, vertex - 256.0 * vertex_high, value)
            mine = (slot_of_lane == rank) & (lane // 16 == e)
            values.append(jnp.where(mine, value, 0.0).astype(BF16))
            owner_rows.append(rows[k])

    for o in range(0, owners, TILE):
        total = jnp.zeros((TILE, LANES), F32)
        for row, value in zip(owner_rows, values):
            total += dot(one_hot_of_row(row, TILE, float(o)), value)
        rows_ref[CAP, o : o + TILE, :] = total.astype(BF16)
    gather_slots(table_ref, rows_ref.at[CAP], rows_ref, 0, 0, 2)
    by_owner(rows_ref, flat_ref, CAP + 1, CAP + 1)
    pairs_out(pairs_ref, 0, table_ref, pair_ref)


def context_side(pair_ref, table_ref):
    n = pair_ref.shape[0] - 16
    tail = pair_ref[n : n + 16, :].astype(F32)
    row = tail[0:1, :] * 256.0 + tail[1:2, :]
    mine = dot(one_hot_of_col(to_col(row), table_ref.shape[0]), table_ref[...])
    return row, pair_terms_of(mine, pair_ref[0:n, :].astype(F32))


def vertex_side(pairs_ref, episode, table_ref, partner_ref):
    pairs = pairs_ref[episode].astype(F32)
    mine = dot(one_hot_of_col(pairs[:, 0:1], table_ref.shape[0]), table_ref[...])
    theirs = dot(one_hot_of_col(pairs[:, 1:2], partner_ref.shape[0]), partner_ref[...])
    return to_row(pairs[:, 0:1]), pair_terms_of(mine, theirs)


def context_first(
    flat_ref, pair_ref, table_ref, state_ref,
    send_ref, slots_ref, new_ref, new_state_ref, rows_ref, got_ref, turned_ref, terms_ref,
):
    by_slot(flat_ref, got_ref, CAP + 1, CAP + 1)
    slots_ref[...] = got_ref[CAP]
    turn(slots_ref, turned_ref)

    def weigh(s, at, mine):
        there = got_ref[s, pl.ds(at, BLOCK), :].astype(F32)
        terms_ref[s, pl.ds(at, BLOCK), :] = (jax.nn.sigmoid(row_dot(mine, there)) * there).astype(BF16)

    gather_slots(table_ref, slots_ref, rows_ref, 0, 0, 0, weigh)
    row, pair_terms = context_side(pair_ref, table_ref)
    adagrad(
        table_ref, state_ref, new_ref, new_state_ref, turned_ref, terms_ref, lane_of(0, 0, 0), row, pair_terms
    )
    gather_slots(new_ref, slots_ref, rows_ref, CAP, 1, 0)
    by_owner(rows_ref, send_ref, 2 * CAP, 2 * CAP)


def vertex_first(
    flat_ref, sent_ref, pairs_ref, partner_ref, table_ref, state_ref,
    send_ref, rows_ref, got_ref, pair_ref, new_ref, new_state_ref, turned_ref, terms_ref,
):
    by_slot(flat_ref, got_ref, 2 * CAP, 2 * CAP)
    turn(sent_ref.at[CAP], turned_ref)
    weigh_slots(sent_ref, 0, got_ref, 0, terms_ref)
    row, pair_terms = vertex_side(pairs_ref, 0, table_ref, partner_ref)
    adagrad(
        table_ref, state_ref, new_ref, new_state_ref, turned_ref, terms_ref, lane_of(0, 0, 2), row, pair_terms
    )
    gather_slots(new_ref, sent_ref.at[CAP], rows_ref, 0, 1, 2)
    by_owner(rows_ref, send_ref, CAP, CAP + 1)
    pairs_out(pairs_ref, 1, new_ref, pair_ref)


def vertex_last(
    got_ref, rows_ref, sent_ref, pairs_ref, partner_ref, table_ref, state_ref, slots_ref, context_ref,
    new_ref, new_state_ref, context_rows_ref, context_turned_ref, turned_ref, terms_ref,
):
    gather_slots(context_ref, slots_ref, context_rows_ref, 0, 1, 0)
    turn(slots_ref, context_turned_ref)
    turn(sent_ref.at[CAP], turned_ref)
    weigh_slots(rows_ref, 0, got_ref, CAP, terms_ref)
    row, pair_terms = vertex_side(pairs_ref, 1, table_ref, partner_ref)
    adagrad(
        table_ref, state_ref, new_ref, new_state_ref, turned_ref, terms_ref, lane_of(1, 0, 2), row, pair_terms
    )


def context_last(
    flat_ref, rows_ref, turned_ref, pair_ref, table_ref, state_ref, new_ref, new_state_ref, got_ref, terms_ref
):
    by_slot(flat_ref, got_ref, CAP, CAP + 1)
    weigh_slots(rows_ref, 0, got_ref, 0, terms_ref)
    row, pair_terms = context_side(pair_ref, table_ref)
    adagrad(
        table_ref, state_ref, new_ref, new_state_ref, turned_ref, terms_ref, lane_of(1, 0, 0), row, pair_terms
    )


def call(kernel, name, outs, scratch, *args):
    return pl.pallas_call(
        kernel,
        name=name,
        out_shape=[jax.ShapeDtypeStruct(s, d) for s, d in outs],
        scratch_shapes=scratch,
        compiler_params=pltpu.CompilerParams(vmem_limit_bytes=24 * 1024 * 1024),
        cost_estimate=pl.CostEstimate(flops=600_000_000, bytes_accessed=4_000_000, transcendentals=2000),
    )(*args)


def exchange(flat, n):
    shape = flat.shape
    per = shape[0] // n
    sub = 2 if per % 4 else 4
    split = flat.reshape(n, per // sub, sub, shape[1]) if per > sub else flat.reshape(n, per, shape[1])
    return lax.all_to_all(split, AXES, split_axis=0, concat_axis=0, tiled=True).reshape(shape)


def passed_along(block, distance, n_devices):
    return lax.ppermute(block, AXES, [((i - distance) % n_devices, i) for i in range(n_devices)])


def body(
    vertex_table, context_table, vertex_state, context_state, pair_blocks, pair_offsets, negative_owner, negative_row
):
    n_type = lax.axis_size("type")
    n = lax.axis_size("dom") * n_type
    rows, width = vertex_table.shape
    episodes, block_pairs, per_block, negatives = negative_owner.shape
    n_pairs = block_pairs * per_block
    shifts = [1 + n_type * (e + 1) for e in range(episodes)]
    pairs = (pair_blocks[:, :, None, :] * TILE + pair_offsets).reshape(episodes, n_pairs, 2)
    owner = negative_owner.reshape(episodes, n_pairs, negatives)
    target = negative_row.reshape(episodes, n_pairs, negatives)
    v_state = vertex_state.reshape(rows // TILE, TILE)
    c_state = context_state.reshape(rows // TILE, TILE)

    table = ((rows, width), BF16)
    state = ((rows // TILE, TILE), F32)
    pair_rows = ((n_pairs + 16, width), BF16)

    def flat(slots):
        return ((n * slots, width), BF16)

    def slots(number):
        return ((number, n, width), BF16)

    turned = pltpu.VMEM((LANES, n), F32)
    terms = pltpu.VMEM((CAP, n, width), BF16)

    flat_a, rows_a, pair_a = call(
        first_kernel, "slots", [flat(CAP + 1), slots(CAP + 1), pair_rows], [], owner, target, pairs, vertex_table
    )
    context_table, pair_a, flat_a = lax.optimization_barrier((context_table, pair_a, flat_a))
    partner_0 = passed_along(context_table, shifts[0], n)
    got_pair_a = passed_along(pair_a, n - shifts[0], n)
    got_a = exchange(flat_a, n)
    got_a, got_pair_a, partner_0 = lax.optimization_barrier((got_a, got_pair_a, partner_0))
    flat_b, slots_b, context_1, c_state_1 = call(
        context_first, "context_first", [flat(2 * CAP), ((n, LANES), BF16), table, state],
        [pltpu.VMEM((2 * CAP, n, width), BF16), pltpu.VMEM((CAP + 1, n, width), BF16), turned, terms],
        got_a, got_pair_a, context_table, c_state,
    )
    partner_1 = passed_along(context_1, shifts[1], n)
    got_b = exchange(flat_b, n)
    got_b, partner_1 = lax.optimization_barrier((got_b, partner_1))
    flat_c, rows_c, rows_got_b, pair_c, vertex_1, v_state_1 = call(
        vertex_first, "vertex_first", [flat(CAP + 1), slots(CAP), slots(2 * CAP), pair_rows, table, state],
        [turned, terms],
        got_b, rows_a, pairs, partner_0, vertex_table, v_state,
    )
    got_pair_c = passed_along(pair_c, n - shifts[1], n)
    got_c = exchange(flat_c, n)
    vertex_2, v_state_2, rows_b, turned_b = call(
        vertex_last, "vertex_last", [table, state, slots(CAP), ((LANES, n), F32)], [turned, terms],
        rows_got_b, rows_c, rows_a, pairs, partner_1, vertex_1, v_state_1, slots_b, context_1,
    )
    context_2, c_state_2 = call(
        context_last, "context_last", [table, state], [pltpu.VMEM((CAP, n, width), BF16), terms],
        got_c, rows_b, turned_b, got_pair_c, context_1, c_state_1,
    )
    return vertex_2, context_2, v_state_2.reshape(rows), c_state_2.reshape(rows)


def solution(mesh):
    in_specs = (
        P(AXES, None),
        P(AXES, None),
        P(AXES),
        P(AXES),
        P(None, AXES, None),
        P(None, AXES, None, None),
        P(None, AXES, None, None),
        P(None, AXES, None, None),
    )
    out_specs = (P(AXES, None), P(AXES, None), P(AXES), P(AXES))
    return jax.shard_map(body, mesh=mesh, in_specs=in_specs, out_specs=out_specs, check_vma=False)
```

```python
import jax
import jax.numpy as jnp
from jax import lax
from jax.experimental import pallas as pl
from jax.experimental.pallas import tpu as pltpu
from jax.sharding import PartitionSpec as P

AXES = ("dom", "type")
TILE = 128
CAP = 3
PART = 64
BLOCK = 128
LANES = 128
F32 = jnp.float32
BF16 = jnp.bfloat16


def iota(shape, dim):
    return lax.broadcasted_iota(jnp.int32, shape, dim)


def fiota(shape, dim):
    return iota(shape, dim).astype(F32)


def ones_where(mask):
    return jnp.where(mask, 1.0, 0.0).astype(BF16)


def dot(a, b):
    return jnp.dot(a, b, preferred_element_type=F32)


def eye():
    return iota((LANES, LANES), 0) == iota((LANES, LANES), 1)


def to_row(col):
    return jnp.sum(jnp.where(eye(), col, 0.0), axis=0, keepdims=True)


def to_col(row):
    return jnp.sum(jnp.where(eye(), row, 0.0), axis=1, keepdims=True)


def one_hot_of_col(col, rows):
    return ones_where(col == fiota((col.shape[0], rows), 1))


def one_hot_of_row(row, rows, first):
    return ones_where(row == fiota((rows, row.shape[1]), 0) + first)


def lane_of(episode, slot, part):
    return 16 * episode + 4 * slot + part


def slot_col(table, lane):
    return table[:, lane : lane + 1] * 256.0 + table[:, lane + 1 : lane + 2] - 1.0


def slot_row(turned_ref, lane):
    return turned_ref[lane : lane + 1, :] * 256.0 + turned_ref[lane + 1 : lane + 2, :] - 1.0


def row_dot(a, b):
    return jnp.sum(a * b, axis=1, keepdims=True)


def blocks(n, size, step):
    for b in range(n // size):
        step(b * size, b)


def by_owner(slots_ref, flat_ref, slots, group):
    j = iota((group * PART, slots * PART), 1)
    move = ones_where(iota((group * PART, slots * PART), 0) == (j % PART) * group + j // PART)

    def step(at, b):
        rows = jnp.concatenate([slots_ref[s, pl.ds(at, PART), :] for s in range(slots)], axis=0)
        flat_ref[pl.ds(at * group, group * PART), :] = dot(move, rows).astype(BF16)

    blocks(slots_ref.shape[1], PART, step)


def by_slot(flat_ref, slots_ref, slots, group):
    i = iota((slots * PART, group * PART), 0)
    move = ones_where(iota((slots * PART, group * PART), 1) == (i % PART) * group + i // PART)

    def step(at, b):
        rows = dot(move, flat_ref[pl.ds(at * group, group * PART), :]).astype(BF16)
        for s in range(slots):
            slots_ref[s, pl.ds(at, PART), :] = rows[s * PART : (s + 1) * PART, :]

    blocks(slots_ref.shape[1], PART, step)


def turn(table_ref, turned_ref):
    for o in range(0, table_ref.shape[0], TILE):
        turned_ref[:, o : o + TILE] = jnp.transpose(table_ref[o : o + TILE, :].astype(F32))


def gather_slots(table_ref, slots_ref, out_ref, first_out, episode, part, after=None):
    def step(at, b):
        slots = slots_ref[pl.ds(at, BLOCK), :].astype(F32)
        for s in range(CAP):
            col = slot_col(slots, lane_of(episode, s, part))
            rows = dot(one_hot_of_col(col, table_ref.shape[0]), table_ref[...])
            out_ref[first_out + s, pl.ds(at, BLOCK), :] = rows.astype(BF16)
            if after:
                after(s, at, rows)

    blocks(slots_ref.shape[0], BLOCK, step)


def weigh_slots(here_ref, first_here, there_ref, first_there, out_ref):
    def step(at, b):
        for s in range(CAP):
            here = here_ref[first_here + s, pl.ds(at, BLOCK), :].astype(F32)
            there = there_ref[first_there + s, pl.ds(at, BLOCK), :].astype(F32)
            out_ref[s, pl.ds(at, BLOCK), :] = (jax.nn.sigmoid(row_dot(here, there)) * there).astype(BF16)

    blocks(out_ref.shape[1], BLOCK, step)


def adagrad(
    table_ref, state_ref, new_ref, new_state_ref, turned_ref, terms_ref, lane0, pair_row, pair_terms
):
    width = table_ref.shape[1]
    index = [slot_row(turned_ref, lane0 + 4 * s) for s in range(CAP)]

    def step(at, b):
        first = jnp.asarray(at).astype(F32)
        grad = dot(one_hot_of_row(pair_row, TILE, first), pair_terms)
        for s in range(CAP):
            grad += dot(one_hot_of_row(index[s], TILE, first), terms_ref[s])
        state = jnp.transpose(jnp.broadcast_to(state_ref[pl.ds(b, 1), :], (TILE, TILE)))
        state = state + row_dot(grad, grad) * (1.0 / width)
        rows = table_ref[pl.ds(at, TILE), :].astype(F32) - 0.5 * grad / jnp.sqrt(state)
        new_ref[pl.ds(at, TILE), :] = rows.astype(BF16)
        new_state_ref[pl.ds(b, 1), :] = jnp.transpose(state)[0:1, :]

    blocks(table_ref.shape[0], TILE, step)


def pairs_out(pairs_ref, episode, table_ref, out_ref):
    n = pairs_ref.shape[0]
    pairs = pairs_ref[:, 2 * episode : 2 * episode + 2]
    rows = dot(one_hot_of_col(pairs[:, 0:1], table_ref.shape[0]), table_ref[...])
    out_ref[0:n, :] = rows.astype(BF16)
    high = jnp.floor(pairs[:, 1:2] * (1.0 / 256.0))
    low = pairs[:, 1:2] - high * 256.0
    which = iota((16, LANES), 0)
    tail = jnp.where(which == 0, to_row(high), jnp.where(which == 1, to_row(low), 0.0))
    out_ref[n : n + 16, :] = tail.astype(BF16)


def pair_terms_of(here, there):
    return ((jax.nn.sigmoid(row_dot(here, there)) - 1.0) * there).astype(BF16)


def columns_of(grids):
    high_part, groups = LANES // 8, []
    spread = ones_where(iota((LANES, 8), 0) // high_part == iota((LANES, 8), 1))
    keep = iota((LANES, LANES), 1) % high_part == iota((LANES, LANES), 0) % high_part
    collect = ones_where(iota((LANES, LANES), 0) // high_part == iota((LANES, LANES), 1))
    for g in range(0, len(grids), 8):
        wide = jnp.concatenate(grids[g : g + 8], axis=1)
        high = jnp.floor(wide * (1.0 / 256.0))
        total = 0.0
        for digit, scale in ((high, 256.0), (wide - 256.0 * high, 1.0)):
            kept = jnp.where(keep, dot(spread, digit.astype(BF16)), 0.0).astype(BF16)
            total = total + scale * dot(kept, collect)
        groups.append(total)
    return [groups[i // 8][:, i % 8 : i % 8 + 1] for i in range(len(grids))]


def first_kernel(owner_ref, row_ref, block_ref, offset_ref, table_ref, flat_ref, rows_ref, pair_ref, pairs_ref):
    episodes, negatives = owner_ref.shape[:2]
    pairs = pairs_ref.shape[0]
    owners = rows_ref.shape[1]
    lane = iota((pairs, LANES), 1)
    part = lane % 4
    slot_of_lane = ((lane // 4) % 4).astype(F32)
    earlier = iota((pairs, pairs), 1) < iota((pairs, pairs), 0)
    grids = [r[e, k].astype(F32) for r in (owner_ref, row_ref) for e in range(episodes) for k in range(negatives)]
    grids += [offset_ref[e, :, w, :].astype(F32) for e in range(episodes) for w in range(2)]
    columns = columns_of(grids)
    wide = jnp.zeros((pairs, LANES), F32)
    for e in range(episodes):
        for w in range(2):
            which = block_ref[e, w : w + 1, :].astype(F32)
            here = iota((pairs, 8), 1) == iota((pairs, 8), 0) // (pairs // 8)
            block = jnp.sum(jnp.where(here, which, 0.0), axis=1, keepdims=True)
            column = block * float(TILE) + columns[2 * episodes * negatives + 2 * e + w]
            wide = jnp.where(lane == 2 * e + w, column, wide)
    pairs_ref[...] = wide
    owner_rows, values = [], []
    for e in range(episodes):
        vertex = wide[:, 2 * e : 2 * e + 1] + 1.0
        vertex_high = jnp.floor(vertex * (1.0 / 256.0))
        cols = columns[e * negatives : (e + 1) * negatives]
        rows = [to_row(c) for c in cols]
        for k in range(negatives):
            same = jnp.where((cols[k] == rows[k]) & earlier, 1.0, 0.0)
            for j in range(k):
                same += jnp.where(cols[k] == rows[j], 1.0, 0.0)
            rank = jnp.sum(same, axis=1, keepdims=True)
            target = columns[(episodes + e) * negatives + k] + 1.0
            target_high = jnp.floor(target * (1.0 / 256.0))
            value = jnp.where(part == 0, target_high, target - 256.0 * target_high)
            value = jnp.where(part == 2, vertex_high, value)
            value = jnp.where(part == 3, vertex - 256.0 * vertex_high, value)
            mine = (slot_of_lane == rank) & (lane // 16 == e)
            values.append(jnp.where(mine, value, 0.0).astype(BF16))
            owner_rows.append(rows[k])

    for o in range(0, owners, TILE):
        total = jnp.zeros((TILE, LANES), F32)
        for row, value in zip(owner_rows, values):
            total += dot(one_hot_of_row(row, TILE, float(o)), value)
        rows_ref[CAP, o : o + TILE, :] = total.astype(BF16)
    gather_slots(table_ref, rows_ref.at[CAP], rows_ref, 0, 0, 2)
    by_owner(rows_ref, flat_ref, CAP + 1, CAP + 1)
    pairs_out(pairs_ref, 0, table_ref, pair_ref)


def context_side(pair_ref, table_ref):
    n = pair_ref.shape[0] - 16
    tail = pair_ref[n : n + 16, :].astype(F32)
    row = tail[0:1, :] * 256.0 + tail[1:2, :]
    mine = dot(one_hot_of_col(to_col(row), table_ref.shape[0]), table_ref[...])
    return row, pair_terms_of(mine, pair_ref[0:n, :].astype(F32))


def vertex_side(pairs_ref, episode, table_ref, partner_ref):
    pairs = pairs_ref[:, 2 * episode : 2 * episode + 2]
    mine = dot(one_hot_of_col(pairs[:, 0:1], table_ref.shape[0]), table_ref[...])
    theirs = dot(one_hot_of_col(pairs[:, 1:2], partner_ref.shape[0]), partner_ref[...])
    return to_row(pairs[:, 0:1]), pair_terms_of(mine, theirs)


def context_first(
    flat_ref, pair_ref, table_ref, state_ref,
    send_ref, slots_ref, new_ref, new_state_ref, rows_ref, got_ref, turned_ref, terms_ref,
):
    by_slot(flat_ref, got_ref, CAP + 1, CAP + 1)
    slots_ref[...] = got_ref[CAP]
    turn(slots_ref, turned_ref)

    def weigh(s, at, mine):
        there = got_ref[s, pl.ds(at, BLOCK), :].astype(F32)
        terms_ref[s, pl.ds(at, BLOCK), :] = (jax.nn.sigmoid(row_dot(mine, there)) * there).astype(BF16)

    gather_slots(table_ref, slots_ref, rows_ref, 0, 0, 0, weigh)
    row, pair_terms = context_side(pair_ref, table_ref)
    adagrad(
        table_ref, state_ref, new_ref, new_state_ref, turned_ref, terms_ref, lane_of(0, 0, 0), row, pair_terms
    )
    gather_slots(new_ref, slots_ref, rows_ref, CAP, 1, 0)
    by_owner(rows_ref, send_ref, 2 * CAP, 2 * CAP)


def vertex_first(
    flat_ref, sent_ref, pairs_ref, partner_ref, table_ref, state_ref,
    send_ref, rows_ref, got_ref, pair_ref, new_ref, new_state_ref, turned_ref, terms_ref,
):
    by_slot(flat_ref, got_ref, 2 * CAP, 2 * CAP)
    turn(sent_ref.at[CAP], turned_ref)
    weigh_slots(sent_ref, 0, got_ref, 0, terms_ref)
    row, pair_terms = vertex_side(pairs_ref, 0, table_ref, partner_ref)
    adagrad(
        table_ref, state_ref, new_ref, new_state_ref, turned_ref, terms_ref, lane_of(0, 0, 2), row, pair_terms
    )
    gather_slots(new_ref, sent_ref.at[CAP], rows_ref, 0, 1, 2)
    by_owner(rows_ref, send_ref, CAP, CAP + 1)
    pairs_out(pairs_ref, 1, new_ref, pair_ref)


def vertex_last(
    got_ref, rows_ref, sent_ref, pairs_ref, partner_ref, table_ref, state_ref, slots_ref, context_ref,
    new_ref, new_state_ref, context_rows_ref, context_turned_ref, turned_ref, terms_ref,
):
    gather_slots(context_ref, slots_ref, context_rows_ref, 0, 1, 0)
    turn(slots_ref, context_turned_ref)
    turn(sent_ref.at[CAP], turned_ref)
    weigh_slots(rows_ref, 0, got_ref, CAP, terms_ref)
    row, pair_terms = vertex_side(pairs_ref, 1, table_ref, partner_ref)
    adagrad(
        table_ref, state_ref, new_ref, new_state_ref, turned_ref, terms_ref, lane_of(1, 0, 2), row, pair_terms
    )


def context_last(
    flat_ref, rows_ref, turned_ref, pair_ref, table_ref, state_ref, new_ref, new_state_ref, got_ref, terms_ref
):
    by_slot(flat_ref, got_ref, CAP, CAP + 1)
    weigh_slots(rows_ref, 0, got_ref, 0, terms_ref)
    row, pair_terms = context_side(pair_ref, table_ref)
    adagrad(
        table_ref, state_ref, new_ref, new_state_ref, turned_ref, terms_ref, lane_of(1, 0, 0), row, pair_terms
    )


def call(kernel, name, outs, scratch, *args, mib=24):
    return pl.pallas_call(
        kernel,
        name=name,
        out_shape=[jax.ShapeDtypeStruct(s, d) for s, d in outs],
        scratch_shapes=scratch,
        compiler_params=pltpu.CompilerParams(vmem_limit_bytes=mib * 1024 * 1024),
        cost_estimate=pl.CostEstimate(flops=600_000_000, bytes_accessed=4_000_000, transcendentals=2000),
    )(*args)


def exchange(flat, n):
    shape = flat.shape
    per = shape[0] // n
    sub = 2 if per % 4 else 4
    split = flat.reshape(n, per // sub, sub, shape[1]) if per > sub else flat.reshape(n, per, shape[1])
    return lax.all_to_all(split, AXES, split_axis=0, concat_axis=0, tiled=True).reshape(shape)


def passed_along(block, distance, n_devices):
    return lax.ppermute(block, AXES, [((i - distance) % n_devices, i) for i in range(n_devices)])


def body(
    vertex_table, context_table, vertex_state, context_state, pair_blocks, pair_offsets, negative_owner, negative_row
):
    n_type = lax.axis_size("type")
    n = lax.axis_size("dom") * n_type
    rows, width = vertex_table.shape
    episodes, block_pairs, per_block, negatives = negative_owner.shape
    n_pairs = block_pairs * per_block
    shifts = [1 + n_type * (e + 1) for e in range(episodes)]
    owner = negative_owner.transpose(0, 3, 1, 2)
    target = negative_row.transpose(0, 3, 1, 2)
    block = pair_blocks.transpose(0, 2, 1)
    offset = pair_offsets.transpose(0, 1, 3, 2)
    v_state = vertex_state.reshape(rows // TILE, TILE)
    c_state = context_state.reshape(rows // TILE, TILE)

    table = ((rows, width), BF16)
    state = ((rows // TILE, TILE), F32)
    pair_rows = ((n_pairs + 16, width), BF16)

    def flat(slots):
        return ((n * slots, width), BF16)

    def slots(number):
        return ((number, n, width), BF16)

    turned = pltpu.VMEM((LANES, n), F32)
    terms = pltpu.VMEM((CAP, n, width), BF16)

    flat_a, rows_a, pair_a, pairs = call(
        first_kernel, "slots", [flat(CAP + 1), slots(CAP + 1), pair_rows, ((n_pairs, LANES), F32)], [],
        owner, target, block, offset, vertex_table, mib=60,
    )
    context_table, pair_a, flat_a = lax.optimization_barrier((context_table, pair_a, flat_a))
    partner_0 = passed_along(context_table, shifts[0], n)
    got_pair_a = passed_along(pair_a, n - shifts[0], n)
    got_a = exchange(flat_a, n)
    got_a, got_pair_a, partner_0 = lax.optimization_barrier((got_a, got_pair_a, partner_0))
    flat_b, slots_b, context_1, c_state_1 = call(
        context_first, "context_first", [flat(2 * CAP), ((n, LANES), BF16), table, state],
        [pltpu.VMEM((2 * CAP, n, width), BF16), pltpu.VMEM((CAP + 1, n, width), BF16), turned, terms],
        got_a, got_pair_a, context_table, c_state,
    )
    partner_1 = passed_along(context_1, shifts[1], n)
    got_b = exchange(flat_b, n)
    got_b, partner_1 = lax.optimization_barrier((got_b, partner_1))
    flat_c, rows_c, rows_got_b, pair_c, vertex_1, v_state_1 = call(
        vertex_first, "vertex_first", [flat(CAP + 1), slots(CAP), slots(2 * CAP), pair_rows, table, state],
        [turned, terms],
        got_b, rows_a, pairs, partner_0, vertex_table, v_state,
    )
    got_pair_c = passed_along(pair_c, n - shifts[1], n)
    got_c = exchange(flat_c, n)
    vertex_2, v_state_2, rows_b, turned_b = call(
        vertex_last, "vertex_last", [table, state, slots(CAP), ((LANES, n), F32)], [turned, terms],
        rows_got_b, rows_c, rows_a, pairs, partner_1, vertex_1, v_state_1, slots_b, context_1,
    )
    context_2, c_state_2 = call(
        context_last, "context_last", [table, state], [pltpu.VMEM((CAP, n, width), BF16), terms],
        got_c, rows_b, turned_b, got_pair_c, context_1, c_state_1,
    )
    return vertex_2, context_2, v_state_2.reshape(rows), c_state_2.reshape(rows)


def solution(mesh):
    in_specs = (
        P(AXES, None),
        P(AXES, None),
        P(AXES),
        P(AXES),
        P(None, AXES, None),
        P(None, AXES, None, None),
        P(None, AXES, None, None),
        P(None, AXES, None, None),
    )
    out_specs = (P(AXES, None), P(AXES, None), P(AXES), P(AXES))
    return jax.shard_map(body, mesh=mesh, in_specs=in_specs, out_specs=out_specs, check_vma=False)
```

```python
import jax
import jax.numpy as jnp
from jax import lax
from jax.experimental import pallas as pl
from jax.experimental.pallas import tpu as pltpu
from jax.sharding import PartitionSpec as P

AXES = ("dom", "type")
TILE = 128
CAP = 3
PART = 64
BLOCK = 128
LANES = 128
F32 = jnp.float32
BF16 = jnp.bfloat16


def iota(shape, dim):
    return lax.broadcasted_iota(jnp.int32, shape, dim)


def fiota(shape, dim):
    return iota(shape, dim).astype(F32)


def ones_where(mask):
    return jnp.where(mask, 1.0, 0.0).astype(BF16)


def dot(a, b):
    return jnp.dot(a, b, preferred_element_type=F32)


def eye():
    return iota((LANES, LANES), 0) == iota((LANES, LANES), 1)


def to_row(col):
    return jnp.sum(jnp.where(eye(), col, 0.0), axis=0, keepdims=True)


def to_col(row):
    return jnp.sum(jnp.where(eye(), row, 0.0), axis=1, keepdims=True)


def short(x):
    return x.astype(jnp.int32).astype(jnp.int16)


def one_hot_of_col(col, rows):
    at = lax.broadcasted_iota(jnp.int16, (col.shape[0], rows), 1)
    return jnp.where(short(col) == at, BF16(1), BF16(0))


def one_hot_of_row(row, rows, first):
    at = lax.broadcasted_iota(jnp.int16, (rows, row.shape[1]), 0)
    return jnp.where(short(row - first) == at, BF16(1), BF16(0))


def lane_of(episode, slot, part):
    return 16 * episode + 4 * slot + part


def slot_col(table, lane):
    return table[:, lane : lane + 1] * 256.0 + table[:, lane + 1 : lane + 2] - 1.0


def slot_row(turned_ref, lane):
    return turned_ref[lane : lane + 1, :] * 256.0 + turned_ref[lane + 1 : lane + 2, :] - 1.0


def row_dot(a, b):
    return jnp.sum(a * b, axis=1, keepdims=True)


def blocks(n, size, step):
    for b in range(n // size):
        step(b * size, b)


def by_owner(slots_ref, flat_ref, slots, group):
    j = iota((group * PART, slots * PART), 1)
    move = ones_where(iota((group * PART, slots * PART), 0) == (j % PART) * group + j // PART)

    def step(at, b):
        rows = jnp.concatenate([slots_ref[s, pl.ds(at, PART), :] for s in range(slots)], axis=0)
        flat_ref[pl.ds(at * group, group * PART), :] = dot(move, rows).astype(BF16)

    blocks(slots_ref.shape[1], PART, step)


def by_slot(flat_ref, slots_ref, slots, group):
    i = iota((slots * PART, group * PART), 0)
    move = ones_where(iota((slots * PART, group * PART), 1) == (i % PART) * group + i // PART)

    def step(at, b):
        rows = dot(move, flat_ref[pl.ds(at * group, group * PART), :]).astype(BF16)
        for s in range(slots):
            slots_ref[s, pl.ds(at, PART), :] = rows[s * PART : (s + 1) * PART, :]

    blocks(slots_ref.shape[1], PART, step)


def turn(table_ref, turned_ref):
    for o in range(0, table_ref.shape[0], TILE):
        turned_ref[:, o : o + TILE] = jnp.transpose(table_ref[o : o + TILE, :].astype(F32))


def gather_slots(table_ref, slots_ref, out_ref, first_out, episode, part, after=None):
    def step(at, b):
        slots = slots_ref[pl.ds(at, BLOCK), :].astype(F32)
        for s in range(CAP):
            col = slot_col(slots, lane_of(episode, s, part))
            rows = dot(one_hot_of_col(col, table_ref.shape[0]), table_ref[...])
            out_ref[first_out + s, pl.ds(at, BLOCK), :] = rows.astype(BF16)
            if after:
                after(s, at, rows)

    blocks(slots_ref.shape[0], BLOCK, step)


def weigh_slots(here_ref, first_here, there_ref, first_there, out_ref):
    def step(at, b):
        for s in range(CAP):
            here = here_ref[first_here + s, pl.ds(at, BLOCK), :].astype(F32)
            there = there_ref[first_there + s, pl.ds(at, BLOCK), :].astype(F32)
            out_ref[s, pl.ds(at, BLOCK), :] = (jax.nn.sigmoid(row_dot(here, there)) * there).astype(BF16)

    blocks(out_ref.shape[1], BLOCK, step)


def adagrad(
    table_ref, state_ref, new_ref, new_state_ref, turned_ref, terms_ref, lane0, pair_row, pair_terms
):
    width = table_ref.shape[1]
    index = [slot_row(turned_ref, lane0 + 4 * s) for s in range(CAP)]

    def step(at, b):
        first = jnp.asarray(at).astype(F32)
        grad = dot(one_hot_of_row(pair_row, TILE, first), pair_terms)
        for s in range(CAP):
            grad += dot(one_hot_of_row(index[s], TILE, first), terms_ref[s])
        state = jnp.transpose(jnp.broadcast_to(state_ref[pl.ds(b, 1), :], (TILE, TILE)))
        state = state + row_dot(grad, grad) * (1.0 / width)
        rows = table_ref[pl.ds(at, TILE), :].astype(F32) - 0.5 * grad / jnp.sqrt(state)
        new_ref[pl.ds(at, TILE), :] = rows.astype(BF16)
        new_state_ref[pl.ds(b, 1), :] = jnp.transpose(state)[0:1, :]

    blocks(table_ref.shape[0], TILE, step)


def numbers_of(pairs_ref, episode):
    column = pairs_ref[0:LANES, 2 * episode + 1 : 2 * episode + 2]
    high = jnp.floor(column * (1.0 / 256.0))
    which = iota((16, LANES), 0)
    low = column - high * 256.0
    return jnp.where(which == 0, to_row(high), jnp.where(which == 1, to_row(low), 0.0)).astype(BF16)


def rows_of(column, table_ref):
    return dot(one_hot_of_col(column, table_ref.shape[0]), table_ref[...])


def pair_terms_of(here, there):
    return ((jax.nn.sigmoid(row_dot(here, there)) - 1.0) * there).astype(BF16)


def columns_of(grids):
    high_part, groups = LANES // 8, []
    spread = ones_where(iota((LANES, 8), 0) // high_part == iota((LANES, 8), 1))
    keep = iota((LANES, LANES), 1) % high_part == iota((LANES, LANES), 0) % high_part
    collect = ones_where(iota((LANES, LANES), 0) // high_part == iota((LANES, LANES), 1))
    for g in range(0, len(grids), 8):
        wide = jnp.concatenate(grids[g : g + 8], axis=1)
        high = jnp.floor(wide * (1.0 / 256.0))
        total = 0.0
        for digit, scale in ((high, 256.0), (wide - 256.0 * high, 1.0)):
            kept = jnp.where(keep, dot(spread, digit.astype(BF16)), 0.0).astype(BF16)
            total = total + scale * dot(kept, collect)
        groups.append(total)
    return [groups[i // 8][:, i % 8 : i % 8 + 1] for i in range(len(grids))]


def first_kernel(
    owner_ref, row_ref, block_ref, offset_ref, table_ref, vertex_state_ref, context_state_ref,
    flat_ref, rows_ref, pair_ref, pairs_ref, numbers_ref,
):
    episodes, negatives = owner_ref.shape[:2]
    pairs = pair_ref.shape[0] - 16
    owners = rows_ref.shape[1]
    lane = iota((pairs, LANES), 1)
    part = lane % 4
    slot_of_lane = ((lane // 4) % 4).astype(F32)
    earlier = iota((pairs, pairs), 1) < iota((pairs, pairs), 0)
    grids = [r[e, k].astype(F32) for r in (owner_ref, row_ref) for e in range(episodes) for k in range(negatives)]
    grids += [offset_ref[e, :, w, :].astype(F32) for e in range(episodes) for w in range(2)]
    columns = columns_of(grids)
    wide = jnp.zeros((pairs, LANES), F32)
    for e in range(episodes):
        for w in range(2):
            which = block_ref[e, w : w + 1, :].astype(F32)
            here = iota((pairs, 8), 1) == iota((pairs, 8), 0) // (pairs // 8)
            block = jnp.sum(jnp.where(here, which, 0.0), axis=1, keepdims=True)
            column = block * float(TILE) + columns[2 * episodes * negatives + 2 * e + w]
            wide = jnp.where(lane == 2 * e + w, column, wide)
    pairs_ref[0:pairs, :] = wide
    pairs_ref[pairs : pairs + 16, :] = jnp.zeros((16, LANES), F32)
    tiles = vertex_state_ref.shape[0]
    pairs_ref[pairs : pairs + tiles, :] = vertex_state_ref[...]
    pairs_ref[pairs + 8 : pairs + 8 + tiles, :] = context_state_ref[...]
    owner_rows, values = [], []
    for e in range(episodes):
        vertex = wide[:, 2 * e : 2 * e + 1] + 1.0
        vertex_high = jnp.floor(vertex * (1.0 / 256.0))
        cols = columns[e * negatives : (e + 1) * negatives]
        rows = [to_row(c) for c in cols]
        for k in range(negatives):
            same = jnp.where((cols[k] == rows[k]) & earlier, 1.0, 0.0)
            for j in range(k):
                same += jnp.where(cols[k] == rows[j], 1.0, 0.0)
            rank = jnp.sum(same, axis=1, keepdims=True)
            target = columns[(episodes + e) * negatives + k] + 1.0
            target_high = jnp.floor(target * (1.0 / 256.0))
            value = jnp.where(part == 0, target_high, target - 256.0 * target_high)
            value = jnp.where(part == 2, vertex_high, value)
            value = jnp.where(part == 3, vertex - 256.0 * vertex_high, value)
            mine = (slot_of_lane == rank) & (lane // 16 == e)
            values.append(jnp.where(mine, value, 0.0).astype(BF16))
            owner_rows.append(rows[k])

    owner_row, value = jnp.concatenate(owner_rows, axis=1), jnp.concatenate(values, axis=0)
    for o in range(0, owners, TILE):
        total = dot(one_hot_of_row(owner_row, TILE, float(o)), value)
        rows_ref[CAP, o : o + TILE, :] = total.astype(BF16)
    gather_slots(table_ref, rows_ref.at[CAP], rows_ref, 0, 0, 2)
    by_owner(rows_ref, flat_ref, CAP + 1, CAP + 1)
    pair_ref[0:pairs, :] = rows_of(wide[:, 0:1], table_ref).astype(BF16)
    pair_ref[pairs : pairs + 16, :] = numbers_of(pairs_ref, 0)
    numbers_ref[...] = numbers_of(pairs_ref, 1)


def row_numbers(digits):
    digits = digits.astype(F32)
    return digits[0:1, :] * 256.0 + digits[1:2, :]


def vertex_side(pairs_ref, episode, table_ref, theirs_ref):
    column = pairs_ref[0:LANES, 2 * episode : 2 * episode + 1]
    return to_row(column), pair_terms_of(rows_of(column, table_ref), theirs_ref[...].astype(F32))


def context_first(
    flat_ref, pair_ref, numbers_ref, table_ref, pairs_ref,
    send_ref, slots_ref, new_ref, new_state_ref, pair_0_ref, pair_1_ref,
    rows_ref, got_ref, turned_ref, terms_ref,
):
    state_ref = pairs_ref.at[LANES + 8 : LANES + 16]
    by_slot(flat_ref, got_ref, CAP + 1, CAP + 1)
    slots_ref[...] = got_ref[CAP]
    turn(slots_ref, turned_ref)

    def weigh(s, at, mine):
        there = got_ref[s, pl.ds(at, BLOCK), :].astype(F32)
        terms_ref[s, pl.ds(at, BLOCK), :] = (jax.nn.sigmoid(row_dot(mine, there)) * there).astype(BF16)

    gather_slots(table_ref, slots_ref, rows_ref, 0, 0, 0, weigh)
    n = pair_ref.shape[0] - 16
    row = row_numbers(pair_ref[n : n + 16, :])
    mine = rows_of(to_col(row), table_ref)
    pair_0_ref[...] = mine.astype(BF16)
    pair_terms = pair_terms_of(mine, pair_ref[0:n, :].astype(F32))
    adagrad(
        table_ref, state_ref, new_ref, new_state_ref, turned_ref, terms_ref, lane_of(0, 0, 0), row, pair_terms
    )
    pair_1_ref[...] = rows_of(to_col(row_numbers(numbers_ref[...])), new_ref).astype(BF16)
    gather_slots(new_ref, slots_ref, rows_ref, CAP, 1, 0)
    by_owner(rows_ref, send_ref, 2 * CAP, 2 * CAP)


def vertex_first(
    flat_ref, sent_ref, pairs_ref, partner_ref, table_ref,
    send_ref, rows_ref, got_ref, pair_ref, new_ref, new_state_ref, turned_ref, terms_ref,
):
    state_ref = pairs_ref.at[LANES : LANES + 8]
    by_slot(flat_ref, got_ref, 2 * CAP, 2 * CAP)
    turn(sent_ref.at[CAP], turned_ref)
    weigh_slots(sent_ref, 0, got_ref, 0, terms_ref)
    row, pair_terms = vertex_side(pairs_ref, 0, table_ref, partner_ref)
    adagrad(
        table_ref, state_ref, new_ref, new_state_ref, turned_ref, terms_ref, lane_of(0, 0, 2), row, pair_terms
    )
    gather_slots(new_ref, sent_ref.at[CAP], rows_ref, 0, 1, 2)
    by_owner(rows_ref, send_ref, CAP, CAP + 1)
    pair_ref[...] = rows_of(pairs_ref[0:LANES, 2:3], new_ref).astype(BF16)


def vertex_last(
    got_ref, rows_ref, sent_ref, pairs_ref, partner_ref, table_ref, state_ref, slots_ref, context_ref,
    new_ref, new_state_ref, context_rows_ref, context_turned_ref, turned_ref, terms_ref,
):
    gather_slots(context_ref, slots_ref, context_rows_ref, 0, 1, 0)
    turn(slots_ref, context_turned_ref)
    turn(sent_ref.at[CAP], turned_ref)
    weigh_slots(rows_ref, 0, got_ref, CAP, terms_ref)
    row, pair_terms = vertex_side(pairs_ref, 1, table_ref, partner_ref)
    adagrad(
        table_ref, state_ref, new_ref, new_state_ref, turned_ref, terms_ref, lane_of(1, 0, 2), row, pair_terms
    )


def context_last(
    flat_ref, rows_ref, turned_ref, pair_ref, numbers_ref, mine_ref, table_ref, state_ref,
    new_ref, new_state_ref, got_ref, terms_ref,
):
    by_slot(flat_ref, got_ref, CAP, CAP + 1)
    weigh_slots(rows_ref, 0, got_ref, 0, terms_ref)
    row = row_numbers(numbers_ref[...])
    pair_terms = pair_terms_of(mine_ref[...].astype(F32), pair_ref[...].astype(F32))
    adagrad(
        table_ref, state_ref, new_ref, new_state_ref, turned_ref, terms_ref, lane_of(1, 0, 0), row, pair_terms
    )


def call(kernel, name, outs, scratch, *args, mib=24):
    return pl.pallas_call(
        kernel,
        name=name,
        out_shape=[jax.ShapeDtypeStruct(s, d) for s, d in outs],
        scratch_shapes=scratch,
        compiler_params=pltpu.CompilerParams(vmem_limit_bytes=mib * 1024 * 1024),
        cost_estimate=pl.CostEstimate(flops=600_000_000, bytes_accessed=4_000_000, transcendentals=2000),
    )(*args)


def exchange(flat, n):
    shape = flat.shape
    per = shape[0] // n
    sub = 2 if per % 4 else 4
    split = flat.reshape(n, per // sub, sub, shape[1]) if per > sub else flat.reshape(n, per, shape[1])
    return lax.all_to_all(split, AXES, split_axis=0, concat_axis=0, tiled=True).reshape(shape)


def passed_along(block, distance, n_devices):
    return lax.ppermute(block, AXES, [((i - distance) % n_devices, i) for i in range(n_devices)])


def body(
    vertex_table, context_table, vertex_state, context_state, pair_blocks, pair_offsets, negative_owner, negative_row
):
    n_type = lax.axis_size("type")
    n = lax.axis_size("dom") * n_type
    rows, width = vertex_table.shape
    episodes, block_pairs, per_block, negatives = negative_owner.shape
    n_pairs = block_pairs * per_block
    shifts = [1 + n_type * (e + 1) for e in range(episodes)]
    owner = negative_owner.transpose(0, 3, 1, 2)
    target = negative_row.transpose(0, 3, 1, 2)
    block = pair_blocks.transpose(0, 2, 1)
    offset = pair_offsets.transpose(0, 1, 3, 2)
    v_state = vertex_state.reshape(rows // TILE, TILE)
    c_state = context_state.reshape(rows // TILE, TILE)

    table = ((rows, width), BF16)
    state = ((rows // TILE, TILE), F32)

    def flat(slots):
        return ((n * slots, width), BF16)

    def slots(number):
        return ((number, n, width), BF16)

    turned = pltpu.VMEM((LANES, n), F32)
    terms = pltpu.VMEM((CAP, n, width), BF16)

    pair_rows = ((n_pairs, width), BF16)
    assert n_pairs == LANES
    flat_a, rows_a, pair_a, pairs, numbers = call(
        first_kernel, "slots",
        [flat(CAP + 1), slots(CAP + 1), ((n_pairs + 16, width), BF16), ((n_pairs + 16, LANES), F32), ((16, LANES), BF16)],
        [], owner, target, block, offset, vertex_table, v_state, c_state, mib=60,
    )
    got_pair_a = passed_along(pair_a, n - shifts[0], n)
    got_numbers = passed_along(numbers, n - shifts[1], n)
    got_a = exchange(flat_a, n)
    flat_b, slots_b, context_1, c_state_1, pair_b0, pair_b1 = call(
        context_first, "context_first",
        [flat(2 * CAP), ((n, LANES), BF16), table, state, pair_rows, pair_rows],
        [pltpu.VMEM((2 * CAP, n, width), BF16), pltpu.VMEM((CAP + 1, n, width), BF16), turned, terms],
        got_a, got_pair_a, got_numbers, context_table, pairs,
    )
    theirs_0 = passed_along(pair_b0, shifts[0], n)
    theirs_1 = passed_along(pair_b1, shifts[1], n)
    got_b = exchange(flat_b, n)
    got_b, theirs_0, theirs_1 = lax.optimization_barrier((got_b, theirs_0, theirs_1))
    flat_c, rows_c, rows_got_b, pair_c, vertex_1, v_state_1 = call(
        vertex_first, "vertex_first", [flat(CAP + 1), slots(CAP), slots(2 * CAP), pair_rows, table, state],
        [turned, terms],
        got_b, rows_a, pairs, theirs_0, vertex_table,
    )
    got_pair_c = passed_along(pair_c, n - shifts[1], n)
    got_c = exchange(flat_c, n)
    vertex_2, v_state_2, rows_b, turned_b = call(
        vertex_last, "vertex_last", [table, state, slots(CAP), ((LANES, n), F32)], [turned, terms],
        rows_got_b, rows_c, rows_a, pairs, theirs_1, vertex_1, v_state_1, slots_b, context_1,
    )
    context_2, c_state_2 = call(
        context_last, "context_last", [table, state], [pltpu.VMEM((CAP, n, width), BF16), terms],
        got_c, rows_b, turned_b, got_pair_c, got_numbers, pair_b1, context_1, c_state_1,
    )
    return vertex_2, context_2, v_state_2.reshape(rows), c_state_2.reshape(rows)


def solution(mesh):
    in_specs = (
        P(AXES, None),
        P(AXES, None),
        P(AXES),
        P(AXES),
        P(None, AXES, None),
        P(None, AXES, None, None),
        P(None, AXES, None, None),
        P(None, AXES, None, None),
    )
    out_specs = (P(AXES, None), P(AXES, None), P(AXES), P(AXES))
    return jax.shard_map(body, mesh=mesh, in_specs=in_specs, out_specs=out_specs, check_vma=False)
```

```python
import jax
import jax.numpy as jnp
from jax import lax
from jax.experimental import pallas as pl
from jax.experimental.pallas import tpu as pltpu
from jax.sharding import PartitionSpec as P

AXES = ("dom", "type")
TILE = 128
CAP = 3
BLOCK = 128
LANES = 128
F32 = jnp.float32
BF16 = jnp.bfloat16


def iota(shape, dim):
    return lax.broadcasted_iota(jnp.int32, shape, dim)


def fiota(shape, dim):
    return iota(shape, dim).astype(F32)


def ones_where(mask):
    return jnp.where(mask, 1.0, 0.0).astype(BF16)


def dot(a, b):
    return jnp.dot(a, b, preferred_element_type=F32)


def eye():
    return iota((LANES, LANES), 0) == iota((LANES, LANES), 1)


def to_row(col):
    return jnp.sum(jnp.where(eye(), col, 0.0), axis=0, keepdims=True)


def to_col(row):
    return jnp.sum(jnp.where(eye(), row, 0.0), axis=1, keepdims=True)


def short(x):
    return x.astype(jnp.int32).astype(jnp.int16)


def one_hot_of_col(col, rows):
    at = lax.broadcasted_iota(jnp.int16, (col.shape[0], rows), 1)
    return jnp.where(short(col) == at, BF16(1), BF16(0))


def one_hot_of_row(row, rows, first):
    at = lax.broadcasted_iota(jnp.int16, (rows, row.shape[1]), 0)
    return jnp.where(short(row - first) == at, BF16(1), BF16(0))


def lane_of(episode, slot, part):
    return 16 * episode + 4 * slot + part


def slot_col(table, lane):
    return table[:, lane : lane + 1] * 256.0 + table[:, lane + 1 : lane + 2] - 1.0


def slot_row(turned_ref, lane):
    return turned_ref[lane : lane + 1, :] * 256.0 + turned_ref[lane + 1 : lane + 2, :] - 1.0


def row_dot(a, b):
    return jnp.sum(a * b, axis=1, keepdims=True)


def blocks(n, size, step):
    for b in range(n // size):
        step(b * size, b)


def part_of(group):
    return 64 if group <= 4 else 32


def by_owner(slots_ref, flat_ref, slots, group):
    part = part_of(group)
    j = iota((group * part, slots * part), 1)
    move = ones_where(iota((group * part, slots * part), 0) == (j % part) * group + j // part)

    def step(at, b):
        rows = jnp.concatenate([slots_ref[s, pl.ds(at, part), :] for s in range(slots)], axis=0)
        flat_ref[pl.ds(at * group, group * part), :] = dot(move, rows).astype(BF16)

    blocks(slots_ref.shape[1], part, step)


def by_slot(flat_ref, slots_ref, first, slots, group):
    part = part_of(group)
    i = iota((slots * part, group * part), 0)
    move = ones_where(iota((slots * part, group * part), 1) == (i % part) * group + i // part + first)

    def step(at, b):
        rows = dot(move, flat_ref[pl.ds(at * group, group * part), :]).astype(BF16)
        for s in range(slots):
            slots_ref[s, pl.ds(at, part), :] = rows[s * part : (s + 1) * part, :]

    blocks(slots_ref.shape[1], part, step)


def turn(table_ref, turned_ref):
    for o in range(0, table_ref.shape[0], TILE):
        turned_ref[:, o : o + TILE] = jnp.transpose(table_ref[o : o + TILE, :].astype(F32))


def gather_slots(table_ref, slots_ref, out_ref, first_out, episode, part, after=None):
    def step(at, b):
        slots = slots_ref[pl.ds(at, BLOCK), :].astype(F32)
        for s in range(CAP):
            col = slot_col(slots, lane_of(episode, s, part))
            rows = dot(one_hot_of_col(col, table_ref.shape[0]), table_ref[...])
            out_ref[first_out + s, pl.ds(at, BLOCK), :] = rows.astype(BF16)
            if after:
                after(s, at, rows)

    blocks(slots_ref.shape[0], BLOCK, step)


def weigh_slots(here_ref, first_here, there_ref, first_there, out_ref):
    def step(at, b):
        for s in range(CAP):
            here = here_ref[first_here + s, pl.ds(at, BLOCK), :].astype(F32)
            there = there_ref[first_there + s, pl.ds(at, BLOCK), :].astype(F32)
            out_ref[s, pl.ds(at, BLOCK), :] = (jax.nn.sigmoid(row_dot(here, there)) * there).astype(BF16)

    blocks(out_ref.shape[1], BLOCK, step)


def scattered(turned_ref, terms_ref, lane0):
    index = [slot_row(turned_ref, lane0 + 4 * s) for s in range(CAP)]

    def grad_of(at, grad):
        for s in range(CAP):
            grad += dot(one_hot_of_row(index[s], TILE, float(at)), terms_ref[s])
        return grad

    return grad_of


def adagrad(table_ref, state_ref, new_ref, new_state_ref, grad_of, pair_row, pair_terms):
    width = table_ref.shape[1]

    def step(at, b):
        grad = grad_of(at, dot(one_hot_of_row(pair_row, TILE, float(at)), pair_terms))
        state = jnp.transpose(jnp.broadcast_to(state_ref[pl.ds(b, 1), :], (TILE, TILE)))
        state = state + row_dot(grad, grad) * (1.0 / width)
        rows = table_ref[pl.ds(at, TILE), :].astype(F32) - 0.5 * grad / jnp.sqrt(state)
        new_ref[pl.ds(at, TILE), :] = rows.astype(BF16)
        new_state_ref[pl.ds(b, 1), :] = jnp.transpose(state)[0:1, :]

    blocks(table_ref.shape[0], TILE, step)


def numbers_of(pairs_ref, episode):
    column = pairs_ref[0:LANES, 2 * episode + 1 : 2 * episode + 2]
    high = jnp.floor(column * (1.0 / 256.0))
    which = iota((16, LANES), 0)
    low = column - high * 256.0
    return jnp.where(which == 0, to_row(high), jnp.where(which == 1, to_row(low), 0.0)).astype(BF16)


def rows_of(column, table_ref):
    return dot(one_hot_of_col(column, table_ref.shape[0]), table_ref[...])


def pair_terms_of(here, there):
    return ((jax.nn.sigmoid(row_dot(here, there)) - 1.0) * there).astype(BF16)


def columns_of(grids):
    high_part, groups = LANES // 8, []
    spread = ones_where(iota((LANES, 8), 0) // high_part == iota((LANES, 8), 1))
    keep = iota((LANES, LANES), 1) % high_part == iota((LANES, LANES), 0) % high_part
    collect = ones_where(iota((LANES, LANES), 0) // high_part == iota((LANES, LANES), 1))
    for g in range(0, len(grids), 8):
        wide = jnp.concatenate(grids[g : g + 8], axis=1)
        high = jnp.floor(wide * (1.0 / 256.0))
        total = 0.0
        for digit, scale in ((high, 256.0), (wide - 256.0 * high, 1.0)):
            kept = jnp.where(keep, dot(spread, digit.astype(BF16)), 0.0).astype(BF16)
            total = total + scale * dot(kept, collect)
        groups.append(total)
    return [groups[i // 8][:, i % 8 : i % 8 + 1] for i in range(len(grids))]


def first_kernel(
    owner_ref, row_ref, block_ref, offset_ref, table_ref, vertex_state_ref, context_state_ref,
    flat_ref, rows_ref, pair_ref, pairs_ref, numbers_ref,
):
    episodes, negatives = owner_ref.shape[:2]
    pairs = pair_ref.shape[0] - 16
    owners = rows_ref.shape[1]
    lane = iota((pairs, LANES), 1)
    part = lane % 4
    slot_of_lane = ((lane // 4) % 4).astype(F32)
    earlier = iota((pairs, pairs), 1) < iota((pairs, pairs), 0)
    grids = [r[e, k].astype(F32) for r in (owner_ref, row_ref) for e in range(episodes) for k in range(negatives)]
    grids += [offset_ref[e, :, w, :].astype(F32) for e in range(episodes) for w in range(2)]
    columns = columns_of(grids)
    wide = jnp.zeros((pairs, LANES), F32)
    for e in range(episodes):
        for w in range(2):
            which = block_ref[e, w : w + 1, :].astype(F32)
            here = iota((pairs, 8), 1) == iota((pairs, 8), 0) // (pairs // 8)
            block = jnp.sum(jnp.where(here, which, 0.0), axis=1, keepdims=True)
            column = block * float(TILE) + columns[2 * episodes * negatives + 2 * e + w]
            wide = jnp.where(lane == 2 * e + w, column, wide)
    pairs_ref[0:pairs, :] = wide
    pairs_ref[pairs : pairs + 16, :] = jnp.zeros((16, LANES), F32)
    tiles = vertex_state_ref.shape[0]
    pairs_ref[pairs : pairs + tiles, :] = vertex_state_ref[...]
    pairs_ref[pairs + 8 : pairs + 8 + tiles, :] = context_state_ref[...]
    owner_rows, values = [], []
    for e in range(episodes):
        vertex = wide[:, 2 * e : 2 * e + 1] + 1.0
        vertex_high = jnp.floor(vertex * (1.0 / 256.0))
        cols = columns[e * negatives : (e + 1) * negatives]
        rows = [to_row(c) for c in cols]
        for k in range(negatives):
            same = jnp.where((cols[k] == rows[k]) & earlier, 1.0, 0.0)
            for j in range(k):
                same += jnp.where(cols[k] == rows[j], 1.0, 0.0)
            rank = jnp.sum(same, axis=1, keepdims=True)
            target = columns[(episodes + e) * negatives + k] + 1.0
            target_high = jnp.floor(target * (1.0 / 256.0))
            value = jnp.where(part == 0, target_high, target - 256.0 * target_high)
            value = jnp.where(part == 2, vertex_high, value)
            value = jnp.where(part == 3, vertex - 256.0 * vertex_high, value)
            mine = (slot_of_lane == rank) & (lane // 16 == e)
            values.append(jnp.where(mine, value, 0.0).astype(BF16))
            owner_rows.append(rows[k])

    owner_row, value = jnp.concatenate(owner_rows, axis=1), jnp.concatenate(values, axis=0)
    for o in range(0, owners, TILE):
        total = dot(one_hot_of_row(owner_row, TILE, float(o)), value)
        rows_ref[CAP, o : o + TILE, :] = total.astype(BF16)
    gather_slots(table_ref, rows_ref.at[CAP], rows_ref, 0, 0, 2)
    by_owner(rows_ref, flat_ref, CAP + 1, CAP + 1)
    pair_ref[0:pairs, :] = rows_of(wide[:, 0:1], table_ref).astype(BF16)
    pair_ref[pairs : pairs + 16, :] = numbers_of(pairs_ref, 0)
    numbers_ref[...] = numbers_of(pairs_ref, 1)


def row_numbers(digits):
    digits = digits.astype(F32)
    return digits[0:1, :] * 256.0 + digits[1:2, :]


def vertex_side(pairs_ref, episode, table_ref, theirs_ref):
    column = pairs_ref[0:LANES, 2 * episode : 2 * episode + 1]
    return to_row(column), pair_terms_of(rows_of(column, table_ref), theirs_ref[...].astype(F32))


def context_first(
    flat_ref, pair_ref, numbers_ref, table_ref, pairs_ref,
    send_ref, slots_ref, new_ref, new_state_ref, pair_0_ref, pair_1_ref,
    rows_ref, got_ref, turned_ref, terms_ref,
):
    state_ref = pairs_ref.at[LANES + 8 : LANES + 16]
    by_slot(flat_ref, got_ref, 0, CAP + 1, CAP + 1)
    slots_ref[...] = got_ref[CAP]
    turn(slots_ref, turned_ref)

    def weigh(s, at, mine):
        there = got_ref[s, pl.ds(at, BLOCK), :].astype(F32)
        terms_ref[s, pl.ds(at, BLOCK), :] = (jax.nn.sigmoid(row_dot(mine, there)) * there).astype(BF16)

    gather_slots(table_ref, slots_ref, rows_ref, 0, 0, 0, weigh)
    n = pair_ref.shape[0] - 16
    row = row_numbers(pair_ref[n : n + 16, :])
    mine = rows_of(to_col(row), table_ref)
    pair_0_ref[...] = mine.astype(BF16)
    pair_terms = pair_terms_of(mine, pair_ref[0:n, :].astype(F32))
    grad_of = scattered(turned_ref, terms_ref, lane_of(0, 0, 0))
    adagrad(table_ref, state_ref, new_ref, new_state_ref, grad_of, row, pair_terms)
    pair_1_ref[...] = rows_of(to_col(row_numbers(numbers_ref[...])), new_ref).astype(BF16)
    gather_slots(new_ref, slots_ref, rows_ref, CAP, 1, 0)
    by_owner(rows_ref, send_ref, 2 * CAP, 2 * CAP)


def vertex_first(
    flat_ref, sent_ref, pairs_ref, partner_ref, table_ref,
    send_ref, pair_ref, new_ref, new_state_ref, turned_ref, rows_ref, got_ref, terms_ref,
):
    state_ref = pairs_ref.at[LANES : LANES + 8]
    by_slot(flat_ref, got_ref, 0, CAP, 2 * CAP)
    turn(sent_ref.at[CAP], turned_ref)
    weigh_slots(sent_ref, 0, got_ref, 0, terms_ref)
    row, pair_terms = vertex_side(pairs_ref, 0, table_ref, partner_ref)
    grad_of = scattered(turned_ref, terms_ref, lane_of(0, 0, 2))
    adagrad(table_ref, state_ref, new_ref, new_state_ref, grad_of, row, pair_terms)
    gather_slots(new_ref, sent_ref.at[CAP], rows_ref, 0, 1, 2)
    by_owner(rows_ref, send_ref, CAP, CAP + 1)
    pair_ref[...] = rows_of(pairs_ref[0:LANES, 2:3], new_ref).astype(BF16)


def vertex_last(
    flat_ref, sent_ref, pairs_ref, partner_ref, table_ref, state_ref, slots_ref, context_ref,
    new_ref, new_state_ref, context_flat_ref, place_ref,
    got_ref, rows_ref, context_turned_ref, turned_ref, terms_ref,
):
    gather_slots(context_ref, slots_ref, rows_ref, 0, 1, 0)
    by_owner(rows_ref, context_flat_ref, CAP, CAP + 1)
    turn(slots_ref, context_turned_ref)
    group = CAP + 1
    part = part_of(group)
    i = iota((CAP * part, group * part), 0)
    move = ones_where(iota((CAP * part, group * part), 1) == (i % part) * group + i // part)
    lanes = [lane_of(1, s, 0) for s in range(CAP)]

    def step(at, b):
        digits = [
            jnp.concatenate([context_turned_ref[k + d : k + d + 1, at : at + part] for k in lanes], axis=1)
            for d in range(2)
        ]
        which = iota((16, CAP * part), 0)
        both = jnp.where(which == 0, digits[0], jnp.where(which == 1, digits[1], 0.0)).astype(BF16)
        moved = dot(both, move)
        place_ref[:, at * group : (at + part) * group] = moved[0:1, :] * 256.0 + moved[1:2, :] - 1.0

    blocks(slots_ref.shape[0], part, step)

    turn(sent_ref.at[CAP], turned_ref)
    by_slot(flat_ref, got_ref, CAP, CAP, 2 * CAP)
    gather_slots(table_ref, sent_ref.at[CAP], rows_ref, 0, 1, 2)
    weigh_slots(rows_ref, 0, got_ref, 0, terms_ref)
    row, pair_terms = vertex_side(pairs_ref, 1, table_ref, partner_ref)
    grad_of = scattered(turned_ref, terms_ref, lane_of(1, 0, 2))
    adagrad(table_ref, state_ref, new_ref, new_state_ref, grad_of, row, pair_terms)


def context_last(
    flat_ref, rows_ref, place_ref, pair_ref, numbers_ref, mine_ref, table_ref, state_ref,
    new_ref, new_state_ref, terms_ref,
):
    def weigh(at, b):
        there = flat_ref[pl.ds(at, BLOCK), :].astype(F32)
        weight = jax.nn.sigmoid(row_dot(rows_ref[pl.ds(at, BLOCK), :].astype(F32), there))
        terms_ref[pl.ds(at, BLOCK), :] = (weight * there).astype(BF16)

    blocks(flat_ref.shape[0], BLOCK, weigh)
    row = row_numbers(numbers_ref[...])
    pair_terms = pair_terms_of(mine_ref[...].astype(F32), pair_ref[...].astype(F32))

    def grad_of(at, grad):
        return grad + dot(one_hot_of_row(place_ref[...], TILE, float(at)), terms_ref[...])

    adagrad(table_ref, state_ref, new_ref, new_state_ref, grad_of, row, pair_terms)


def call(kernel, name, outs, scratch, *args, mib=24):
    return pl.pallas_call(
        kernel,
        name=name,
        out_shape=[jax.ShapeDtypeStruct(s, d) for s, d in outs],
        scratch_shapes=scratch,
        compiler_params=pltpu.CompilerParams(vmem_limit_bytes=mib * 1024 * 1024),
        cost_estimate=pl.CostEstimate(flops=600_000_000, bytes_accessed=4_000_000, transcendentals=2000),
    )(*args)


def exchange(flat, n):
    shape = flat.shape
    per = shape[0] // n
    sub = 2 if per % 4 else 4
    split = flat.reshape(n, per // sub, sub, shape[1]) if per > sub else flat.reshape(n, per, shape[1])
    return lax.all_to_all(split, AXES, split_axis=0, concat_axis=0, tiled=True).reshape(shape)


def passed_along(block, distance, n_devices):
    return lax.ppermute(block, AXES, [((i - distance) % n_devices, i) for i in range(n_devices)])


def body(
    vertex_table, context_table, vertex_state, context_state, pair_blocks, pair_offsets, negative_owner, negative_row
):
    n_type = lax.axis_size("type")
    n = lax.axis_size("dom") * n_type
    rows, width = vertex_table.shape
    episodes, block_pairs, per_block, negatives = negative_owner.shape
    n_pairs = block_pairs * per_block
    shifts = [1 + n_type * (e + 1) for e in range(episodes)]
    owner = negative_owner.transpose(0, 3, 1, 2)
    target = negative_row.transpose(0, 3, 1, 2)
    block = pair_blocks.transpose(0, 2, 1)
    offset = pair_offsets.transpose(0, 1, 3, 2)
    v_state = vertex_state.reshape(rows // TILE, TILE)
    c_state = context_state.reshape(rows // TILE, TILE)

    table = ((rows, width), BF16)
    state = ((rows // TILE, TILE), F32)

    def flat(slots):
        return ((n * slots, width), BF16)

    def slots(number):
        return ((number, n, width), BF16)

    turned = pltpu.VMEM((LANES, n), F32)
    terms = pltpu.VMEM((CAP, n, width), BF16)

    pair_rows = ((n_pairs, width), BF16)
    assert n_pairs == LANES
    flat_a, rows_a, pair_a, pairs, numbers = call(
        first_kernel, "slots",
        [flat(CAP + 1), slots(CAP + 1), ((n_pairs + 16, width), BF16), ((n_pairs + 16, LANES), F32), ((16, LANES), BF16)],
        [], owner, target, block, offset, vertex_table, v_state, c_state, mib=60,
    )
    got_pair_a = passed_along(pair_a, n - shifts[0], n)
    got_numbers = passed_along(numbers, n - shifts[1], n)
    got_a = exchange(flat_a, n)
    flat_b, slots_b, context_1, c_state_1, pair_b0, pair_b1 = call(
        context_first, "context_first",
        [flat(2 * CAP), ((n, LANES), BF16), table, state, pair_rows, pair_rows],
        [pltpu.VMEM((2 * CAP, n, width), BF16), pltpu.VMEM((CAP + 1, n, width), BF16), turned, terms],
        got_a, got_pair_a, got_numbers, context_table, pairs,
    )
    theirs_0 = passed_along(pair_b0, shifts[0], n)
    theirs_1 = passed_along(pair_b1, shifts[1], n)
    got_b = exchange(flat_b, n)
    got_b, theirs_0, theirs_1 = lax.optimization_barrier((got_b, theirs_0, theirs_1))
    flat_c, pair_c, vertex_1, v_state_1 = call(
        vertex_first, "vertex_first", [flat(CAP + 1), pair_rows, table, state], [turned, terms, terms, terms],
        got_b, rows_a, pairs, theirs_0, vertex_table,
    )
    got_pair_c = passed_along(pair_c, n - shifts[1], n)
    got_c = exchange(flat_c, n)
    vertex_2, v_state_2, rows_b, place_b = call(
        vertex_last, "vertex_last", [table, state, flat(CAP + 1), ((1, n * (CAP + 1)), F32)],
        [terms, terms, turned, turned, terms],
        got_b, rows_a, pairs, theirs_1, vertex_1, v_state_1, slots_b, context_1,
    )
    context_2, c_state_2 = call(
        context_last, "context_last", [table, state], [pltpu.VMEM((n * (CAP + 1), width), BF16)],
        got_c, rows_b, place_b, got_pair_c, got_numbers, pair_b1, context_1, c_state_1,
    )
    return vertex_2, context_2, v_state_2.reshape(rows), c_state_2.reshape(rows)


def solution(mesh):
    in_specs = (
        P(AXES, None),
        P(AXES, None),
        P(AXES),
        P(AXES),
        P(None, AXES, None),
        P(None, AXES, None, None),
        P(None, AXES, None, None),
        P(None, AXES, None, None),
    )
    out_specs = (P(AXES, None), P(AXES, None), P(AXES), P(AXES))
    return jax.shard_map(body, mesh=mesh, in_specs=in_specs, out_specs=out_specs, check_vma=False)
```

```python
import jax
import jax.numpy as jnp
from jax import lax
from jax.experimental import pallas as pl
from jax.experimental.pallas import tpu as pltpu
from jax.sharding import PartitionSpec as P

AXES = ("dom", "type")
TILE = 128
CAP = 3
BLOCK = 128
LANES = 128
F32 = jnp.float32
BF16 = jnp.bfloat16


def iota(shape, dim):
    return lax.broadcasted_iota(jnp.int32, shape, dim)


def fiota(shape, dim):
    return iota(shape, dim).astype(F32)


def ones_where(mask):
    return jnp.where(mask, 1.0, 0.0).astype(BF16)


def dot(a, b):
    return jnp.dot(a, b, preferred_element_type=F32)


def eye():
    return iota((LANES, LANES), 0) == iota((LANES, LANES), 1)


def to_row(col):
    return jnp.sum(jnp.where(eye(), col, 0.0), axis=0, keepdims=True)


def to_col(row):
    return jnp.sum(jnp.where(eye(), row, 0.0), axis=1, keepdims=True)


def short(x):
    return x.astype(jnp.int32).astype(jnp.int16)


def one_hot_of_col(col, rows):
    at = lax.broadcasted_iota(jnp.int16, (col.shape[0], rows), 1)
    return jnp.where(short(col) == at, BF16(1), BF16(0))


def one_hot_of_row(row, rows, first):
    at = lax.broadcasted_iota(jnp.int16, (rows, row.shape[1]), 0)
    return jnp.where(short(row - first) == at, BF16(1), BF16(0))


def lane_of(episode, slot, part):
    return 16 * episode + 4 * slot + part


def slot_col(table, lane):
    return table[:, lane : lane + 1] * 256.0 + table[:, lane + 1 : lane + 2] - 1.0


def slot_row(turned_ref, lane):
    return turned_ref[lane : lane + 1, :] * 256.0 + turned_ref[lane + 1 : lane + 2, :] - 1.0


def row_dot(a, b):
    return jnp.sum(a * b, axis=1, keepdims=True)


def blocks(n, size, step):
    for b in range(n // size):
        step(b * size, b)


def part_of(group):
    return 64 if group <= 4 else 32


def by_owner(slots_ref, flat_ref, slots, group):
    part = part_of(group)
    j = iota((group * part, slots * part), 1)
    move = ones_where(iota((group * part, slots * part), 0) == (j % part) * group + j // part)

    def step(at, b):
        rows = jnp.concatenate([slots_ref[s, pl.ds(at, part), :] for s in range(slots)], axis=0)
        flat_ref[pl.ds(at * group, group * part), :] = dot(move, rows).astype(BF16)

    blocks(slots_ref.shape[1], part, step)


def by_slot(flat_ref, slots_ref, first, slots, group):
    part = part_of(group)
    i = iota((slots * part, group * part), 0)
    move = ones_where(iota((slots * part, group * part), 1) == (i % part) * group + i // part + first)

    def step(at, b):
        rows = dot(move, flat_ref[pl.ds(at * group, group * part), :]).astype(BF16)
        for s in range(slots):
            slots_ref[s, pl.ds(at, part), :] = rows[s * part : (s + 1) * part, :]

    blocks(slots_ref.shape[1], part, step)


def turn(table_ref, turned_ref):
    for o in range(0, table_ref.shape[0], TILE):
        turned_ref[:, o : o + TILE] = jnp.transpose(table_ref[o : o + TILE, :].astype(F32))


def gather_slots(table_ref, slots_ref, out_ref, first_out, episode, part, after=None):
    def step(at, b):
        slots = slots_ref[pl.ds(at, BLOCK), :].astype(F32)
        for s in range(CAP):
            col = slot_col(slots, lane_of(episode, s, part))
            rows = dot(one_hot_of_col(col, table_ref.shape[0]), table_ref[...])
            out_ref[first_out + s, pl.ds(at, BLOCK), :] = rows.astype(BF16)
            if after:
                after(s, at, rows)

    blocks(slots_ref.shape[0], BLOCK, step)


def weigh_slots(here_ref, first_here, there_ref, first_there, out_ref):
    def step(at, b):
        for s in range(CAP):
            here = here_ref[first_here + s, pl.ds(at, BLOCK), :].astype(F32)
            there = there_ref[first_there + s, pl.ds(at, BLOCK), :].astype(F32)
            out_ref[s, pl.ds(at, BLOCK), :] = (jax.nn.sigmoid(row_dot(here, there)) * there).astype(BF16)

    blocks(out_ref.shape[1], BLOCK, step)


def scattered(turned_ref, terms_ref, lane0):
    index = [slot_row(turned_ref, lane0 + 4 * s) for s in range(CAP)]

    def grad_of(at, grad):
        for s in range(CAP):
            grad += dot(one_hot_of_row(index[s], TILE, float(at)), terms_ref[s])
        return grad

    return grad_of


def adagrad(table_ref, state_ref, new_ref, new_state_ref, grad_of, pair_row, pair_terms):
    width = table_ref.shape[1]

    def step(at, b):
        grad = grad_of(at, dot(one_hot_of_row(pair_row, TILE, float(at)), pair_terms))
        state = jnp.transpose(jnp.broadcast_to(state_ref[pl.ds(b, 1), :], (TILE, TILE)))
        state = state + row_dot(grad, grad) * (1.0 / width)
        rows = table_ref[pl.ds(at, TILE), :].astype(F32) - grad * (0.5 * lax.rsqrt(state))
        new_ref[pl.ds(at, TILE), :] = rows.astype(BF16)
        new_state_ref[pl.ds(b, 1), :] = jnp.transpose(state)[0:1, :]

    blocks(table_ref.shape[0], TILE, step)


def numbers_of(pairs_ref, episode):
    column = pairs_ref[0:LANES, 2 * episode + 1 : 2 * episode + 2]
    high = jnp.floor(column * (1.0 / 256.0))
    which = iota((16, LANES), 0)
    low = column - high * 256.0
    return jnp.where(which == 0, to_row(high), jnp.where(which == 1, to_row(low), 0.0)).astype(BF16)


def rows_of(column, table_ref):
    return dot(one_hot_of_col(column, table_ref.shape[0]), table_ref[...])


def pair_terms_of(here, there):
    return ((jax.nn.sigmoid(row_dot(here, there)) - 1.0) * there).astype(BF16)


def rows_of_grids(grids):
    count, wide = len(grids), LANES // 8
    stack = jnp.concatenate(grids, axis=0)
    repeat = ones_where(iota((wide, LANES), 1) % wide == iota((wide, LANES), 0))
    high = jnp.floor(stack * (1.0 / 256.0))
    low = stack - 256.0 * high
    spread = 256.0 * dot(high.astype(BF16), repeat) + dot(low.astype(BF16), repeat)
    mine = iota((8 * count, LANES), 0) % 8 == iota((8 * count, LANES), 1) // wide
    return jnp.sum(jnp.where(mine, spread, 0.0).reshape(count, 8, LANES), axis=1)


def first_kernel(
    owner_ref, row_ref, block_ref, offset_ref, table_ref, vertex_state_ref, context_state_ref,
    flat_ref, rows_ref, pair_ref, pairs_ref, numbers_ref,
):
    episodes, negatives = owner_ref.shape[:2]
    pairs = pair_ref.shape[0] - 16
    owners = rows_ref.shape[1]
    lane = iota((pairs, LANES), 1)
    part = lane % 4
    slot_of_lane = ((lane // 4) % 4).astype(F32)
    earlier = iota((pairs, pairs), 1) < iota((pairs, pairs), 0)
    grids = [r[e, k].astype(F32) for r in (owner_ref, row_ref) for e in range(episodes) for k in range(negatives)]
    grids += [offset_ref[e, :, w, :].astype(F32) for e in range(episodes) for w in range(2)]
    lines = rows_of_grids(grids)
    of_block = ones_where(iota((8, LANES), 0) == iota((8, LANES), 1) // (LANES // 8))
    blocks_of = jnp.concatenate([block_ref[e].astype(F32) for e in range(episodes)], axis=0)
    n_lists = 2 * episodes * negatives
    offsets = lines[n_lists:] + float(TILE) * dot(blocks_of.astype(BF16), of_block)
    lines = jnp.concatenate([lines[:n_lists], offsets], axis=0)
    turned = jnp.transpose(jnp.concatenate([lines, jnp.zeros((LANES - lines.shape[0], LANES), F32)], axis=0))
    columns = [turned[:, i : i + 1] for i in range(n_lists)]
    wide = turned[:, n_lists : n_lists + 2 * episodes]
    pairs_ref[0:pairs, :] = jnp.zeros((pairs, LANES), F32)
    pairs_ref[0:pairs, 0 : 2 * episodes] = wide
    pairs_ref[pairs : pairs + 16, :] = jnp.zeros((16, LANES), F32)
    tiles = vertex_state_ref.shape[0]
    pairs_ref[pairs : pairs + tiles, :] = vertex_state_ref[...]
    pairs_ref[pairs + 8 : pairs + 8 + tiles, :] = context_state_ref[...]
    vectors = rows_of(wide[:, 0:1], table_ref)
    pair_ref[0:pairs, :] = vectors.astype(BF16)
    owner_rows, values = [], []
    for e in range(episodes):
        vertex = wide[:, 2 * e : 2 * e + 1] + 1.0
        vertex_high = jnp.floor(vertex * (1.0 / 256.0))
        cols = columns[e * negatives : (e + 1) * negatives]
        rows = [lines[e * negatives + k : e * negatives + k + 1, :] for k in range(negatives)]
        for k in range(negatives):
            same = jnp.where((cols[k] == rows[k]) & earlier, 1.0, 0.0)
            for j in range(k):
                same += jnp.where(cols[k] == rows[j], 1.0, 0.0)
            rank = jnp.sum(same, axis=1, keepdims=True)
            target = columns[(episodes + e) * negatives + k] + 1.0
            target_high = jnp.floor(target * (1.0 / 256.0))
            value = jnp.where(part == 0, target_high, target - 256.0 * target_high)
            value = jnp.where(part == 2, vertex_high, value)
            value = jnp.where(part == 3, vertex - 256.0 * vertex_high, value)
            mine = (slot_of_lane == rank) & (lane // 16 == e)
            value = jnp.where(mine, value, 0.0).astype(BF16)
            if e == 0:
                value = [value] + [jnp.where(rank == s, vectors, 0.0).astype(BF16) for s in range(CAP)]
                value = jnp.concatenate(value, axis=1)
            values.append(value)
            owner_rows.append(rows[k])

    hot = [jnp.concatenate(owner_rows[e * negatives : (e + 1) * negatives], axis=1) for e in range(episodes)]
    value = [jnp.concatenate(values[e * negatives : (e + 1) * negatives], axis=0) for e in range(episodes)]
    for o in range(0, owners, TILE):
        first, second = [dot(one_hot_of_row(h, TILE, float(o)), v) for h, v in zip(hot, value)]
        rows_ref[CAP, o : o + TILE, :] = (first[:, 0:LANES] + second).astype(BF16)
        for s in range(CAP):
            rows_ref[s, o : o + TILE, :] = first[:, (s + 1) * LANES : (s + 2) * LANES].astype(BF16)
    by_owner(rows_ref, flat_ref, CAP + 1, CAP + 1)
    pair_ref[pairs : pairs + 16, :] = numbers_of(pairs_ref, 0)
    numbers_ref[...] = numbers_of(pairs_ref, 1)


def row_numbers(digits):
    digits = digits.astype(F32)
    return digits[0:1, :] * 256.0 + digits[1:2, :]


def vertex_side(pairs_ref, episode, table_ref, theirs_ref):
    column = pairs_ref[0:LANES, 2 * episode : 2 * episode + 1]
    return to_row(column), pair_terms_of(rows_of(column, table_ref), theirs_ref[...].astype(F32))


def context_first(
    flat_ref, pair_ref, numbers_ref, table_ref, pairs_ref,
    send_ref, slots_ref, new_ref, new_state_ref, pair_0_ref, pair_1_ref,
    rows_ref, got_ref, turned_ref, terms_ref,
):
    state_ref = pairs_ref.at[LANES + 8 : LANES + 16]
    by_slot(flat_ref, got_ref, 0, CAP + 1, CAP + 1)
    slots_ref[...] = got_ref[CAP]
    turn(slots_ref, turned_ref)

    def weigh(s, at, mine):
        there = got_ref[s, pl.ds(at, BLOCK), :].astype(F32)
        terms_ref[s, pl.ds(at, BLOCK), :] = (jax.nn.sigmoid(row_dot(mine, there)) * there).astype(BF16)

    gather_slots(table_ref, slots_ref, rows_ref, 0, 0, 0, weigh)
    n = pair_ref.shape[0] - 16
    row = row_numbers(pair_ref[n : n + 16, :])
    mine = rows_of(to_col(row), table_ref)
    pair_0_ref[...] = mine.astype(BF16)
    pair_terms = pair_terms_of(mine, pair_ref[0:n, :].astype(F32))
    grad_of = scattered(turned_ref, terms_ref, lane_of(0, 0, 0))
    adagrad(table_ref, state_ref, new_ref, new_state_ref, grad_of, row, pair_terms)
    pair_1_ref[...] = rows_of(to_col(row_numbers(numbers_ref[...])), new_ref).astype(BF16)
    gather_slots(new_ref, slots_ref, rows_ref, CAP, 1, 0)
    by_owner(rows_ref, send_ref, 2 * CAP, 2 * CAP)


def vertex_first(
    flat_ref, sent_ref, pairs_ref, partner_ref, table_ref,
    send_ref, pair_ref, new_ref, new_state_ref, turned_ref, rows_ref, got_ref, terms_ref,
):
    state_ref = pairs_ref.at[LANES : LANES + 8]
    by_slot(flat_ref, got_ref, 0, CAP, 2 * CAP)
    turn(sent_ref.at[CAP], turned_ref)
    weigh_slots(sent_ref, 0, got_ref, 0, terms_ref)
    row, pair_terms = vertex_side(pairs_ref, 0, table_ref, partner_ref)
    grad_of = scattered(turned_ref, terms_ref, lane_of(0, 0, 2))
    adagrad(table_ref, state_ref, new_ref, new_state_ref, grad_of, row, pair_terms)
    gather_slots(new_ref, sent_ref.at[CAP], rows_ref, 0, 1, 2)
    by_owner(rows_ref, send_ref, CAP, CAP + 1)
    pair_ref[...] = rows_of(pairs_ref[0:LANES, 2:3], new_ref).astype(BF16)


def vertex_last(
    flat_ref, sent_ref, pairs_ref, partner_ref, table_ref, state_ref, slots_ref, context_ref,
    new_ref, new_state_ref, context_rows_ref, context_turned_ref,
    got_ref, rows_ref, turned_ref, terms_ref,
):
    gather_slots(context_ref, slots_ref, context_rows_ref, 0, 1, 0)
    turn(slots_ref, context_turned_ref)

    turn(sent_ref.at[CAP], turned_ref)
    by_slot(flat_ref, got_ref, CAP, CAP, 2 * CAP)
    gather_slots(table_ref, sent_ref.at[CAP], rows_ref, 0, 1, 2)
    weigh_slots(rows_ref, 0, got_ref, 0, terms_ref)
    row, pair_terms = vertex_side(pairs_ref, 1, table_ref, partner_ref)
    grad_of = scattered(turned_ref, terms_ref, lane_of(1, 0, 2))
    adagrad(table_ref, state_ref, new_ref, new_state_ref, grad_of, row, pair_terms)


def context_last(
    flat_ref, rows_ref, turned_ref, pair_ref, numbers_ref, mine_ref, table_ref, state_ref,
    new_ref, new_state_ref, got_ref, terms_ref,
):
    by_slot(flat_ref, got_ref, 0, CAP, CAP + 1)
    weigh_slots(rows_ref, 0, got_ref, 0, terms_ref)
    row = row_numbers(numbers_ref[...])
    pair_terms = pair_terms_of(mine_ref[...].astype(F32), pair_ref[...].astype(F32))
    grad_of = scattered(turned_ref, terms_ref, lane_of(1, 0, 0))
    adagrad(table_ref, state_ref, new_ref, new_state_ref, grad_of, row, pair_terms)


def call(kernel, name, outs, scratch, *args, mib=24):
    return pl.pallas_call(
        kernel,
        name=name,
        out_shape=[jax.ShapeDtypeStruct(s, d) for s, d in outs],
        scratch_shapes=scratch,
        compiler_params=pltpu.CompilerParams(vmem_limit_bytes=mib * 1024 * 1024),
        cost_estimate=pl.CostEstimate(flops=600_000_000, bytes_accessed=4_000_000, transcendentals=2000),
    )(*args)


def exchange(flat, n):
    shape = flat.shape
    per = shape[0] // n
    sub = 2 if per % 4 else 4
    split = flat.reshape(n, per // sub, sub, shape[1]) if per > sub else flat.reshape(n, per, shape[1])
    return lax.all_to_all(split, AXES, split_axis=0, concat_axis=0, tiled=True).reshape(shape)


def passed_along(block, distance, n_devices):
    return lax.ppermute(block, AXES, [((i - distance) % n_devices, i) for i in range(n_devices)])


def body(
    vertex_table, context_table, vertex_state, context_state, pair_blocks, pair_offsets, negative_owner, negative_row
):
    n_type = lax.axis_size("type")
    n = lax.axis_size("dom") * n_type
    rows, width = vertex_table.shape
    episodes, block_pairs, per_block, negatives = negative_owner.shape
    n_pairs = block_pairs * per_block
    shifts = [1 + n_type * (e + 1) for e in range(episodes)]
    owner = negative_owner.transpose(0, 3, 1, 2)
    target = negative_row.transpose(0, 3, 1, 2)
    block = pair_blocks.transpose(0, 2, 1)
    offset = pair_offsets.transpose(0, 1, 3, 2)
    v_state = vertex_state.reshape(rows // TILE, TILE)
    c_state = context_state.reshape(rows // TILE, TILE)

    table = ((rows, width), BF16)
    state = ((rows // TILE, TILE), F32)

    def flat(slots):
        return ((n * slots, width), BF16)

    def slots(number):
        return ((number, n, width), BF16)

    turned = pltpu.VMEM((LANES, n), F32)
    terms = pltpu.VMEM((CAP, n, width), BF16)

    pair_rows = ((n_pairs, width), BF16)
    assert n_pairs == LANES
    flat_a, rows_a, pair_a, pairs, numbers = call(
        first_kernel, "slots",
        [flat(CAP + 1), slots(CAP + 1), ((n_pairs + 16, width), BF16), ((n_pairs + 16, LANES), F32), ((16, LANES), BF16)],
        [], owner, target, block, offset, vertex_table, v_state, c_state, mib=60,
    )
    got_pair_a = passed_along(pair_a, n - shifts[0], n)
    got_numbers = passed_along(numbers, n - shifts[1], n)
    got_a = exchange(flat_a, n)
    flat_b, slots_b, context_1, c_state_1, pair_b0, pair_b1 = call(
        context_first, "context_first",
        [flat(2 * CAP), ((n, LANES), BF16), table, state, pair_rows, pair_rows],
        [pltpu.VMEM((2 * CAP, n, width), BF16), pltpu.VMEM((CAP + 1, n, width), BF16), turned, terms],
        got_a, got_pair_a, got_numbers, context_table, pairs,
    )
    theirs_0 = passed_along(pair_b0, shifts[0], n)
    theirs_1 = passed_along(pair_b1, shifts[1], n)
    got_b = exchange(flat_b, n)
    got_b, theirs_0, theirs_1 = lax.optimization_barrier((got_b, theirs_0, theirs_1))
    flat_c, pair_c, vertex_1, v_state_1 = call(
        vertex_first, "vertex_first", [flat(CAP + 1), pair_rows, table, state], [turned, terms, terms, terms],
        got_b, rows_a, pairs, theirs_0, vertex_table,
    )
    got_pair_c = passed_along(pair_c, n - shifts[1], n)
    got_c = exchange(flat_c, n)
    vertex_2, v_state_2, rows_b, turned_b = call(
        vertex_last, "vertex_last", [table, state, slots(CAP), ((LANES, n), F32)], [terms, terms, turned, terms],
        got_b, rows_a, pairs, theirs_1, vertex_1, v_state_1, slots_b, context_1,
    )
    context_2, c_state_2 = call(
        context_last, "context_last", [table, state], [terms, terms],
        got_c, rows_b, turned_b, got_pair_c, got_numbers, pair_b1, context_1, c_state_1,
    )
    return vertex_2, context_2, v_state_2.reshape(rows), c_state_2.reshape(rows)


def solution(mesh):
    in_specs = (
        P(AXES, None),
        P(AXES, None),
        P(AXES),
        P(AXES),
        P(None, AXES, None),
        P(None, AXES, None, None),
        P(None, AXES, None, None),
        P(None, AXES, None, None),
    )
    out_specs = (P(AXES, None), P(AXES, None), P(AXES), P(AXES))
    return jax.shard_map(body, mesh=mesh, in_specs=in_specs, out_specs=out_specs, check_vma=False)
```

```python
import jax
import jax.numpy as jnp
from jax import lax
from jax.experimental import pallas as pl
from jax.experimental.pallas import tpu as pltpu
from jax.sharding import PartitionSpec as P

AXES = ("dom", "type")
TILE = 128
CAP = 3
BLOCK = 128
LANES = 128
F32 = jnp.float32
BF16 = jnp.bfloat16


def iota(shape, dim):
    return lax.broadcasted_iota(jnp.int32, shape, dim)


def fiota(shape, dim):
    return iota(shape, dim).astype(F32)


def ones_where(mask):
    return jnp.where(mask, 1.0, 0.0).astype(BF16)


def dot(a, b):
    return jnp.dot(a, b, preferred_element_type=F32)


def eye():
    return iota((LANES, LANES), 0) == iota((LANES, LANES), 1)


def to_row(col):
    return jnp.sum(jnp.where(eye(), col, 0.0), axis=0, keepdims=True)


def to_col(row):
    return jnp.sum(jnp.where(eye(), row, 0.0), axis=1, keepdims=True)


def short(x):
    return x.astype(jnp.int32).astype(jnp.int16)


def one_hot_of_col(col, rows):
    at = lax.broadcasted_iota(jnp.int16, (col.shape[0], rows), 1)
    return jnp.where(short(col) == at, BF16(1), BF16(0))


def one_hot_of_row(row, rows, first):
    at = lax.broadcasted_iota(jnp.int16, (rows, row.shape[1]), 0)
    return jnp.where(short(row - first) == at, BF16(1), BF16(0))


def lane_of(episode, slot, part):
    return 16 * episode + 4 * slot + part


def slot_col(table, lane):
    return table[:, lane : lane + 1] * 256.0 + table[:, lane + 1 : lane + 2] - 1.0


def slot_row(turned_ref, lane):
    return turned_ref[lane : lane + 1, :] * 256.0 + turned_ref[lane + 1 : lane + 2, :] - 1.0


def row_dot(a, b):
    return jnp.sum(a * b, axis=1, keepdims=True)


def blocks(n, size, step):
    for b in range(n // size):
        step(b * size, b)


def by_owner(slots_ref, flat_ref, wide_ref, slots, group):
    owners = slots_ref.shape[1]
    for s in range(group):
        rows = slots_ref[s].astype(F32) if s < slots else jnp.zeros((owners, flat_ref.shape[1]), F32)
        wide_ref[pl.ds(s, owners, stride=group), :] = rows
    flat_ref[...] = wide_ref[...].astype(BF16)


def by_slot(flat_ref, slots_ref, wide_ref, first, slots, group):
    wide_ref[...] = flat_ref[...].astype(F32)
    for s in range(slots):
        slots_ref[s] = wide_ref[pl.ds(first + s, slots_ref.shape[1], stride=group), :].astype(BF16)


def turn(table_ref, turned_ref):
    for o in range(0, table_ref.shape[0], TILE):
        turned_ref[:, o : o + TILE] = jnp.transpose(table_ref[o : o + TILE, :].astype(F32))


def gather_slots(table_ref, slots_ref, out_ref, first_out, episode, part, after=None):
    def step(at, b):
        slots = slots_ref[pl.ds(at, BLOCK), :].astype(F32)
        for s in range(CAP):
            col = slot_col(slots, lane_of(episode, s, part))
            rows = dot(one_hot_of_col(col, table_ref.shape[0]), table_ref[...])
            out_ref[first_out + s, pl.ds(at, BLOCK), :] = rows.astype(BF16)
            if after:
                after(s, at, rows)

    blocks(slots_ref.shape[0], BLOCK, step)


def weigh_slots(here_ref, first_here, there_ref, first_there, out_ref):
    def step(at, b):
        for s in range(CAP):
            here = here_ref[first_here + s, pl.ds(at, BLOCK), :].astype(F32)
            there = there_ref[first_there + s, pl.ds(at, BLOCK), :].astype(F32)
            out_ref[s, pl.ds(at, BLOCK), :] = (jax.nn.sigmoid(row_dot(here, there)) * there).astype(BF16)

    blocks(out_ref.shape[1], BLOCK, step)


def scattered(turned_ref, terms_ref, lane0):
    index = [slot_row(turned_ref, lane0 + 4 * s) for s in range(CAP)]

    def grad_of(at, grad):
        for s in range(CAP):
            grad += dot(one_hot_of_row(index[s], TILE, float(at)), terms_ref[s])
        return grad

    return grad_of


def adagrad(table_ref, state_ref, new_ref, new_state_ref, grad_of, pair_row, pair_terms):
    width = table_ref.shape[1]

    def step(at, b):
        grad = grad_of(at, dot(one_hot_of_row(pair_row, TILE, float(at)), pair_terms))
        state = jnp.transpose(jnp.broadcast_to(state_ref[pl.ds(b, 1), :], (TILE, TILE)))
        state = state + row_dot(grad, grad) * (1.0 / width)
        rows = table_ref[pl.ds(at, TILE), :].astype(F32) - grad * (0.5 * lax.rsqrt(state))
        new_ref[pl.ds(at, TILE), :] = rows.astype(BF16)
        new_state_ref[pl.ds(b, 1), :] = jnp.transpose(state)[0:1, :]

    blocks(table_ref.shape[0], TILE, step)


def numbers_of(pairs_ref, episode):
    column = pairs_ref[0:LANES, 2 * episode + 1 : 2 * episode + 2]
    high = jnp.floor(column * (1.0 / 256.0))
    which = iota((16, LANES), 0)
    low = column - high * 256.0
    return jnp.where(which == 0, to_row(high), jnp.where(which == 1, to_row(low), 0.0)).astype(BF16)


def rows_of(column, table_ref):
    return dot(one_hot_of_col(column, table_ref.shape[0]), table_ref[...])


def pair_terms_of(here, there):
    return ((jax.nn.sigmoid(row_dot(here, there)) - 1.0) * there).astype(BF16)


def rows_of_grids(grids):
    count, wide = len(grids), LANES // 8
    stack = jnp.concatenate(grids, axis=0)
    repeat = ones_where(iota((wide, LANES), 1) % wide == iota((wide, LANES), 0))
    high = jnp.floor(stack * (1.0 / 256.0))
    low = stack - 256.0 * high
    spread = 256.0 * dot(high.astype(BF16), repeat) + dot(low.astype(BF16), repeat)
    mine = iota((8 * count, LANES), 0) % 8 == iota((8 * count, LANES), 1) // wide
    return jnp.sum(jnp.where(mine, spread, 0.0).reshape(count, 8, LANES), axis=1)


def first_kernel(
    owner_ref, row_ref, block_ref, offset_ref, table_ref, vertex_state_ref, context_state_ref,
    flat_ref, rows_ref, pair_ref, pairs_ref, numbers_ref, wide_ref,
):
    episodes, negatives = owner_ref.shape[:2]
    pairs = pair_ref.shape[0] - 16
    owners = rows_ref.shape[1]
    lane = iota((pairs, LANES), 1)
    part = lane % 4
    slot_of_lane = ((lane // 4) % 4).astype(F32)
    earlier = iota((pairs, pairs), 1) < iota((pairs, pairs), 0)
    grids = [r[e, k].astype(F32) for r in (owner_ref, row_ref) for e in range(episodes) for k in range(negatives)]
    grids += [offset_ref[e, :, w, :].astype(F32) for e in range(episodes) for w in range(2)]
    lines = rows_of_grids(grids)
    of_block = ones_where(iota((8, LANES), 0) == iota((8, LANES), 1) // (LANES // 8))
    blocks_of = jnp.concatenate([block_ref[e].astype(F32) for e in range(episodes)], axis=0)
    n_lists = 2 * episodes * negatives
    offsets = lines[n_lists:] + float(TILE) * dot(blocks_of.astype(BF16), of_block)
    lines = jnp.concatenate([lines[:n_lists], offsets], axis=0)
    turned = jnp.transpose(jnp.concatenate([lines, jnp.zeros((LANES - lines.shape[0], LANES), F32)], axis=0))
    columns = [turned[:, i : i + 1] for i in range(n_lists)]
    wide = turned[:, n_lists : n_lists + 2 * episodes]
    pairs_ref[0:pairs, :] = jnp.zeros((pairs, LANES), F32)
    pairs_ref[0:pairs, 0 : 2 * episodes] = wide
    pairs_ref[pairs : pairs + 16, :] = jnp.zeros((16, LANES), F32)
    tiles = vertex_state_ref.shape[0]
    pairs_ref[pairs : pairs + tiles, :] = vertex_state_ref[...]
    pairs_ref[pairs + 8 : pairs + 8 + tiles, :] = context_state_ref[...]
    vectors = rows_of(wide[:, 0:1], table_ref)
    pair_ref[0:pairs, :] = vectors.astype(BF16)
    owner_rows, values = [], []
    for e in range(episodes):
        vertex = wide[:, 2 * e : 2 * e + 1] + 1.0
        vertex_high = jnp.floor(vertex * (1.0 / 256.0))
        cols = columns[e * negatives : (e + 1) * negatives]
        rows = [lines[e * negatives + k : e * negatives + k + 1, :] for k in range(negatives)]
        for k in range(negatives):
            same = jnp.where((cols[k] == rows[k]) & earlier, 1.0, 0.0)
            for j in range(k):
                same += jnp.where(cols[k] == rows[j], 1.0, 0.0)
            rank = jnp.sum(same, axis=1, keepdims=True)
            target = columns[(episodes + e) * negatives + k] + 1.0
            target_high = jnp.floor(target * (1.0 / 256.0))
            value = jnp.where(part == 0, target_high, target - 256.0 * target_high)
            value = jnp.where(part == 2, vertex_high, value)
            value = jnp.where(part == 3, vertex - 256.0 * vertex_high, value)
            mine = (slot_of_lane == rank) & (lane // 16 == e)
            value = jnp.where(mine, value, 0.0).astype(BF16)
            if e == 0:
                value = [value] + [jnp.where(rank == s, vectors, 0.0).astype(BF16) for s in range(CAP)]
                value = jnp.concatenate(value, axis=1)
            values.append(value)
            owner_rows.append(rows[k])

    hot = [jnp.concatenate(owner_rows[e * negatives : (e + 1) * negatives], axis=1) for e in range(episodes)]
    value = [jnp.concatenate(values[e * negatives : (e + 1) * negatives], axis=0) for e in range(episodes)]
    for o in range(0, owners, TILE):
        first, second = [dot(one_hot_of_row(h, TILE, float(o)), v) for h, v in zip(hot, value)]
        rows_ref[CAP, o : o + TILE, :] = (first[:, 0:LANES] + second).astype(BF16)
        for s in range(CAP):
            rows_ref[s, o : o + TILE, :] = first[:, (s + 1) * LANES : (s + 2) * LANES].astype(BF16)
    by_owner(rows_ref, flat_ref, wide_ref, CAP + 1, CAP + 1)
    pair_ref[pairs : pairs + 16, :] = numbers_of(pairs_ref, 0)
    numbers_ref[...] = numbers_of(pairs_ref, 1)


def row_numbers(digits):
    digits = digits.astype(F32)
    return digits[0:1, :] * 256.0 + digits[1:2, :]


def vertex_side(pairs_ref, episode, table_ref, theirs_ref):
    column = pairs_ref[0:LANES, 2 * episode : 2 * episode + 1]
    return to_row(column), pair_terms_of(rows_of(column, table_ref), theirs_ref[...].astype(F32))


def context_first(
    flat_ref, pair_ref, numbers_ref, table_ref, pairs_ref,
    send_ref, slots_ref, new_ref, new_state_ref, pair_0_ref, pair_1_ref,
    rows_ref, got_ref, turned_ref, terms_ref, wide_ref, got_wide_ref,
):
    state_ref = pairs_ref.at[LANES + 8 : LANES + 16]
    by_slot(flat_ref, got_ref, got_wide_ref, 0, CAP + 1, CAP + 1)
    slots_ref[...] = got_ref[CAP]
    turn(slots_ref, turned_ref)

    def weigh(s, at, mine):
        there = got_ref[s, pl.ds(at, BLOCK), :].astype(F32)
        terms_ref[s, pl.ds(at, BLOCK), :] = (jax.nn.sigmoid(row_dot(mine, there)) * there).astype(BF16)

    gather_slots(table_ref, slots_ref, rows_ref, 0, 0, 0, weigh)
    n = pair_ref.shape[0] - 16
    row = row_numbers(pair_ref[n : n + 16, :])
    mine = rows_of(to_col(row), table_ref)
    pair_0_ref[...] = mine.astype(BF16)
    pair_terms = pair_terms_of(mine, pair_ref[0:n, :].astype(F32))
    grad_of = scattered(turned_ref, terms_ref, lane_of(0, 0, 0))
    adagrad(table_ref, state_ref, new_ref, new_state_ref, grad_of, row, pair_terms)
    pair_1_ref[...] = rows_of(to_col(row_numbers(numbers_ref[...])), new_ref).astype(BF16)
    gather_slots(new_ref, slots_ref, rows_ref, CAP, 1, 0)
    by_owner(rows_ref, send_ref, wide_ref, 2 * CAP, 2 * CAP)


def vertex_first(
    flat_ref, sent_ref, pairs_ref, partner_ref, table_ref,
    send_ref, pair_ref, new_ref, new_state_ref, turned_ref, rows_ref, got_ref, terms_ref, wide_ref, got_wide_ref,
):
    state_ref = pairs_ref.at[LANES : LANES + 8]
    by_slot(flat_ref, got_ref, got_wide_ref, 0, CAP, 2 * CAP)
    turn(sent_ref.at[CAP], turned_ref)
    weigh_slots(sent_ref, 0, got_ref, 0, terms_ref)
    row, pair_terms = vertex_side(pairs_ref, 0, table_ref, partner_ref)
    grad_of = scattered(turned_ref, terms_ref, lane_of(0, 0, 2))
    adagrad(table_ref, state_ref, new_ref, new_state_ref, grad_of, row, pair_terms)
    gather_slots(new_ref, sent_ref.at[CAP], rows_ref, 0, 1, 2)
    by_owner(rows_ref, send_ref, wide_ref, CAP, CAP + 1)
    pair_ref[...] = rows_of(pairs_ref[0:LANES, 2:3], new_ref).astype(BF16)


def vertex_last(
    flat_ref, sent_ref, pairs_ref, partner_ref, table_ref, state_ref, slots_ref, context_ref,
    new_ref, new_state_ref, context_rows_ref, context_turned_ref,
    got_ref, rows_ref, turned_ref, terms_ref, got_wide_ref,
):
    gather_slots(context_ref, slots_ref, context_rows_ref, 0, 1, 0)
    turn(slots_ref, context_turned_ref)

    turn(sent_ref.at[CAP], turned_ref)
    by_slot(flat_ref, got_ref, got_wide_ref, CAP, CAP, 2 * CAP)
    gather_slots(table_ref, sent_ref.at[CAP], rows_ref, 0, 1, 2)
    weigh_slots(rows_ref, 0, got_ref, 0, terms_ref)
    row, pair_terms = vertex_side(pairs_ref, 1, table_ref, partner_ref)
    grad_of = scattered(turned_ref, terms_ref, lane_of(1, 0, 2))
    adagrad(table_ref, state_ref, new_ref, new_state_ref, grad_of, row, pair_terms)


def context_last(
    flat_ref, rows_ref, turned_ref, pair_ref, numbers_ref, mine_ref, table_ref, state_ref,
    new_ref, new_state_ref, got_ref, terms_ref, got_wide_ref,
):
    by_slot(flat_ref, got_ref, got_wide_ref, 0, CAP, CAP + 1)
    weigh_slots(rows_ref, 0, got_ref, 0, terms_ref)
    row = row_numbers(numbers_ref[...])
    pair_terms = pair_terms_of(mine_ref[...].astype(F32), pair_ref[...].astype(F32))
    grad_of = scattered(turned_ref, terms_ref, lane_of(1, 0, 0))
    adagrad(table_ref, state_ref, new_ref, new_state_ref, grad_of, row, pair_terms)


def call(kernel, name, outs, scratch, *args, mib=24):
    return pl.pallas_call(
        kernel,
        name=name,
        out_shape=[jax.ShapeDtypeStruct(s, d) for s, d in outs],
        scratch_shapes=scratch,
        compiler_params=pltpu.CompilerParams(vmem_limit_bytes=mib * 1024 * 1024),
        cost_estimate=pl.CostEstimate(flops=600_000_000, bytes_accessed=4_000_000, transcendentals=2000),
    )(*args)


def exchange(flat, n):
    shape = flat.shape
    per = shape[0] // n
    sub = 2 if per % 4 else 4
    split = flat.reshape(n, per // sub, sub, shape[1]) if per > sub else flat.reshape(n, per, shape[1])
    return lax.all_to_all(split, AXES, split_axis=0, concat_axis=0, tiled=True).reshape(shape)


def passed_along(block, distance, n_devices):
    return lax.ppermute(block, AXES, [((i - distance) % n_devices, i) for i in range(n_devices)])


def body(
    vertex_table, context_table, vertex_state, context_state, pair_blocks, pair_offsets, negative_owner, negative_row
):
    n_type = lax.axis_size("type")
    n = lax.axis_size("dom") * n_type
    rows, width = vertex_table.shape
    episodes, block_pairs, per_block, negatives = negative_owner.shape
    n_pairs = block_pairs * per_block
    shifts = [1 + n_type * (e + 1) for e in range(episodes)]
    owner = negative_owner.transpose(0, 3, 1, 2)
    target = negative_row.transpose(0, 3, 1, 2)
    block = pair_blocks.transpose(0, 2, 1)
    offset = pair_offsets.transpose(0, 1, 3, 2)
    v_state = vertex_state.reshape(rows // TILE, TILE)
    c_state = context_state.reshape(rows // TILE, TILE)

    table = ((rows, width), BF16)
    state = ((rows // TILE, TILE), F32)

    def flat(slots):
        return ((n * slots, width), BF16)

    def slots(number):
        return ((number, n, width), BF16)

    def wide(slots):
        return pltpu.VMEM((n * slots, width), F32)

    turned = pltpu.VMEM((LANES, n), F32)
    terms = pltpu.VMEM((CAP, n, width), BF16)

    pair_rows = ((n_pairs, width), BF16)
    assert n_pairs == LANES
    flat_a, rows_a, pair_a, pairs, numbers = call(
        first_kernel, "slots",
        [flat(CAP + 1), slots(CAP + 1), ((n_pairs + 16, width), BF16), ((n_pairs + 16, LANES), F32), ((16, LANES), BF16)],
        [wide(CAP + 1)], owner, target, block, offset, vertex_table, v_state, c_state, mib=60,
    )
    got_pair_a = passed_along(pair_a, n - shifts[0], n)
    got_numbers = passed_along(numbers, n - shifts[1], n)
    got_a = exchange(flat_a, n)
    flat_b, slots_b, context_1, c_state_1, pair_b0, pair_b1 = call(
        context_first, "context_first",
        [flat(2 * CAP), ((n, LANES), BF16), table, state, pair_rows, pair_rows],
        [pltpu.VMEM((2 * CAP, n, width), BF16), pltpu.VMEM((CAP + 1, n, width), BF16), turned, terms, wide(2 * CAP), wide(CAP + 1)],
        got_a, got_pair_a, got_numbers, context_table, pairs,
    )
    theirs_0 = passed_along(pair_b0, shifts[0], n)
    theirs_1 = passed_along(pair_b1, shifts[1], n)
    got_b = exchange(flat_b, n)
    got_b, theirs_0, theirs_1 = lax.optimization_barrier((got_b, theirs_0, theirs_1))
    flat_c, pair_c, vertex_1, v_state_1 = call(
        vertex_first, "vertex_first", [flat(CAP + 1), pair_rows, table, state],
        [turned, terms, terms, terms, wide(CAP + 1), wide(2 * CAP)],
        got_b, rows_a, pairs, theirs_0, vertex_table,
    )
    got_pair_c = passed_along(pair_c, n - shifts[1], n)
    got_c = exchange(flat_c, n)
    vertex_2, v_state_2, rows_b, turned_b = call(
        vertex_last, "vertex_last", [table, state, slots(CAP), ((LANES, n), F32)],
        [terms, terms, turned, terms, wide(2 * CAP)],
        got_b, rows_a, pairs, theirs_1, vertex_1, v_state_1, slots_b, context_1,
    )
    context_2, c_state_2 = call(
        context_last, "context_last", [table, state], [terms, terms, wide(CAP + 1)],
        got_c, rows_b, turned_b, got_pair_c, got_numbers, pair_b1, context_1, c_state_1,
    )
    return vertex_2, context_2, v_state_2.reshape(rows), c_state_2.reshape(rows)


def solution(mesh):
    in_specs = (
        P(AXES, None),
        P(AXES, None),
        P(AXES),
        P(AXES),
        P(None, AXES, None),
        P(None, AXES, None, None),
        P(None, AXES, None, None),
        P(None, AXES, None, None),
    )
    out_specs = (P(AXES, None), P(AXES, None), P(AXES), P(AXES))
    return jax.shard_map(body, mesh=mesh, in_specs=in_specs, out_specs=out_specs, check_vma=False)
```

```python
import jax
import jax.numpy as jnp
from jax import lax
from jax.experimental import pallas as pl
from jax.experimental.pallas import tpu as pltpu
from jax.sharding import PartitionSpec as P

AXES = ("dom", "type")
TILE = 128
CAP = 3
BLOCK = 128
LANES = 128
F32 = jnp.float32
BF16 = jnp.bfloat16


def iota(shape, dim):
    return lax.broadcasted_iota(jnp.int32, shape, dim)


def fiota(shape, dim):
    return iota(shape, dim).astype(F32)


def ones_where(mask):
    return jnp.where(mask, 1.0, 0.0).astype(BF16)


def dot(a, b):
    return jnp.dot(a, b, preferred_element_type=F32)


def eye():
    return iota((LANES, LANES), 0) == iota((LANES, LANES), 1)


def to_row(col):
    return jnp.sum(jnp.where(eye(), col, 0.0), axis=0, keepdims=True)


def to_col(row):
    return jnp.sum(jnp.where(eye(), row, 0.0), axis=1, keepdims=True)


def short(x):
    return x.astype(jnp.int32).astype(jnp.int16)


def one_hot_of_col(col, rows):
    at = lax.broadcasted_iota(jnp.int16, (col.shape[0], rows), 1)
    return jnp.where(short(col) == at, BF16(1), BF16(0))


def one_hot_of_row(row, rows, first):
    at = lax.broadcasted_iota(jnp.int16, (rows, row.shape[1]), 0)
    return jnp.where(short(row - first) == at, BF16(1), BF16(0))


def lane_of(episode, slot, part):
    return 16 * episode + 4 * slot + part


def slot_col(table, lane):
    return table[:, lane : lane + 1] * 256.0 + table[:, lane + 1 : lane + 2] - 1.0


def slot_row(turned_ref, lane):
    return turned_ref[lane : lane + 1, :] * 256.0 + turned_ref[lane + 1 : lane + 2, :] - 1.0


def row_dot(a, b):
    return jnp.sum(a * b, axis=1, keepdims=True)


def blocks(n, size, step):
    for b in range(n // size):
        step(b * size, b)


def by_owner(slots_ref, flat_ref, wide_ref, slots, group):
    owners = slots_ref.shape[1]
    for s in range(group):
        rows = slots_ref[s].astype(F32) if s < slots else jnp.zeros((owners, flat_ref.shape[1]), F32)
        wide_ref[pl.ds(s, owners, stride=group), :] = rows
    flat_ref[...] = wide_ref[...].astype(BF16)


def by_slot(flat_ref, slots_ref, wide_ref, first, slots, group):
    wide_ref[...] = flat_ref[...].astype(F32)
    for s in range(slots):
        slots_ref[s] = wide_ref[pl.ds(first + s, slots_ref.shape[1], stride=group), :].astype(BF16)


def turn(table_ref, turned_ref):
    for o in range(0, table_ref.shape[0], TILE):
        turned_ref[:, o : o + TILE] = jnp.transpose(table_ref[o : o + TILE, :].astype(F32))


def gather_slots(table_ref, slots_ref, out_ref, first_out, episode, part, after=None):
    def step(at, b):
        slots = slots_ref[pl.ds(at, BLOCK), :].astype(F32)
        for s in range(CAP):
            col = slot_col(slots, lane_of(episode, s, part))
            rows = dot(one_hot_of_col(col, table_ref.shape[0]), table_ref[...])
            out_ref[first_out + s, pl.ds(at, BLOCK), :] = rows.astype(BF16)
            if after:
                after(s, at, rows)

    blocks(slots_ref.shape[0], BLOCK, step)


def weigh_slots(here_ref, first_here, there_ref, first_there, out_ref):
    def step(at, b):
        for s in range(CAP):
            here = here_ref[first_here + s, pl.ds(at, BLOCK), :].astype(F32)
            there = there_ref[first_there + s, pl.ds(at, BLOCK), :].astype(F32)
            out_ref[s, pl.ds(at, BLOCK), :] = (jax.nn.sigmoid(row_dot(here, there)) * there).astype(BF16)

    blocks(out_ref.shape[1], BLOCK, step)


def weigh_flat(here_ref, first_here, flat_ref, wide_ref, group, out_ref):
    wide_ref[...] = flat_ref[...].astype(F32)

    def step(at, b):
        for s in range(CAP):
            here = here_ref[first_here + s, pl.ds(at, BLOCK), :].astype(F32)
            there = wide_ref[pl.ds(at * group + s, BLOCK, stride=group), :]
            out_ref[s, pl.ds(at, BLOCK), :] = (jax.nn.sigmoid(row_dot(here, there)) * there).astype(BF16)

    blocks(out_ref.shape[1], BLOCK, step)


def scattered(turned_ref, terms_ref, lane0):
    index = [slot_row(turned_ref, lane0 + 4 * s) for s in range(CAP)]

    def grad_of(at, grad):
        for s in range(CAP):
            grad += dot(one_hot_of_row(index[s], TILE, float(at)), terms_ref[s])
        return grad

    return grad_of


def adagrad(table_ref, state_ref, new_ref, new_state_ref, grad_of, pair_row, pair_terms):
    width = table_ref.shape[1]

    def step(at, b):
        grad = grad_of(at, dot(one_hot_of_row(pair_row, TILE, float(at)), pair_terms))
        state = jnp.transpose(jnp.broadcast_to(state_ref[pl.ds(b, 1), :], (TILE, TILE)))
        state = state + row_dot(grad, grad) * (1.0 / width)
        rows = table_ref[pl.ds(at, TILE), :].astype(F32) - grad * (0.5 * lax.rsqrt(state))
        new_ref[pl.ds(at, TILE), :] = rows.astype(BF16)
        new_state_ref[pl.ds(b, 1), :] = jnp.transpose(state)[0:1, :]

    blocks(table_ref.shape[0], TILE, step)


def numbers_of(pairs_ref, episode):
    column = pairs_ref[0:LANES, 2 * episode + 1 : 2 * episode + 2]
    high = jnp.floor(column * (1.0 / 256.0))
    which = iota((16, LANES), 0)
    low = column - high * 256.0
    return jnp.where(which == 0, to_row(high), jnp.where(which == 1, to_row(low), 0.0)).astype(BF16)


def rows_of(column, table_ref):
    return dot(one_hot_of_col(column, table_ref.shape[0]), table_ref[...])


def pair_terms_of(here, there):
    return ((jax.nn.sigmoid(row_dot(here, there)) - 1.0) * there).astype(BF16)


def rows_of_grids(grids):
    count, wide = len(grids), LANES // 8
    stack = jnp.concatenate(grids, axis=0)
    repeat = ones_where(iota((wide, LANES), 1) % wide == iota((wide, LANES), 0))
    high = jnp.floor(stack * (1.0 / 256.0))
    low = stack - 256.0 * high
    spread = 256.0 * dot(high.astype(BF16), repeat) + dot(low.astype(BF16), repeat)
    mine = iota((8 * count, LANES), 0) % 8 == iota((8 * count, LANES), 1) // wide
    return jnp.sum(jnp.where(mine, spread, 0.0).reshape(count, 8, LANES), axis=1)


def first_kernel(
    owner_ref, row_ref, block_ref, offset_ref, table_ref, vertex_state_ref, context_state_ref,
    flat_ref, rows_ref, pair_ref, pairs_ref, numbers_ref, wide_ref,
):
    episodes, negatives = owner_ref.shape[:2]
    pairs = pair_ref.shape[0] - 16
    owners = rows_ref.shape[1]
    lane = iota((pairs, LANES), 1)
    part = lane % 4
    slot_of_lane = ((lane // 4) % 4).astype(F32)
    earlier = iota((pairs, pairs), 1) < iota((pairs, pairs), 0)
    grids = [r[e, k].astype(F32) for r in (owner_ref, row_ref) for e in range(episodes) for k in range(negatives)]
    grids += [offset_ref[e, :, w, :].astype(F32) for e in range(episodes) for w in range(2)]
    lines = rows_of_grids(grids)
    of_block = ones_where(iota((8, LANES), 0) == iota((8, LANES), 1) // (LANES // 8))
    blocks_of = jnp.concatenate([block_ref[e].astype(F32) for e in range(episodes)], axis=0)
    n_lists = 2 * episodes * negatives
    offsets = lines[n_lists:] + float(TILE) * dot(blocks_of.astype(BF16), of_block)
    lines = jnp.concatenate([lines[:n_lists], offsets], axis=0)
    turned = jnp.transpose(jnp.concatenate([lines, jnp.zeros((LANES - lines.shape[0], LANES), F32)], axis=0))
    columns = [turned[:, i : i + 1] for i in range(n_lists)]
    wide = turned[:, n_lists : n_lists + 2 * episodes]
    pairs_ref[0:pairs, :] = jnp.zeros((pairs, LANES), F32)
    pairs_ref[0:pairs, 0 : 2 * episodes] = wide
    pairs_ref[pairs : pairs + 16, :] = jnp.zeros((16, LANES), F32)
    tiles = vertex_state_ref.shape[0]
    pairs_ref[pairs : pairs + tiles, :] = vertex_state_ref[...]
    pairs_ref[pairs + 8 : pairs + 8 + tiles, :] = context_state_ref[...]
    vectors = rows_of(wide[:, 0:1], table_ref)
    pair_ref[0:pairs, :] = vectors.astype(BF16)
    owner_rows, values = [], []
    for e in range(episodes):
        vertex = wide[:, 2 * e : 2 * e + 1] + 1.0
        vertex_high = jnp.floor(vertex * (1.0 / 256.0))
        cols = columns[e * negatives : (e + 1) * negatives]
        rows = [lines[e * negatives + k : e * negatives + k + 1, :] for k in range(negatives)]
        for k in range(negatives):
            same = jnp.where((cols[k] == rows[k]) & earlier, 1.0, 0.0)
            for j in range(k):
                same += jnp.where(cols[k] == rows[j], 1.0, 0.0)
            rank = jnp.sum(same, axis=1, keepdims=True)
            target = columns[(episodes + e) * negatives + k] + 1.0
            target_high = jnp.floor(target * (1.0 / 256.0))
            value = jnp.where(part == 0, target_high, target - 256.0 * target_high)
            value = jnp.where(part == 2, vertex_high, value)
            value = jnp.where(part == 3, vertex - 256.0 * vertex_high, value)
            mine = (slot_of_lane == rank) & (lane // 16 == e)
            value = jnp.where(mine, value, 0.0).astype(BF16)
            if e == 0:
                value = [value] + [jnp.where(rank == s, vectors, 0.0).astype(BF16) for s in range(CAP)]
                value = jnp.concatenate(value, axis=1)
            values.append(value)
            owner_rows.append(rows[k])

    hot = [jnp.concatenate(owner_rows[e * negatives : (e + 1) * negatives], axis=1) for e in range(episodes)]
    value = [jnp.concatenate(values[e * negatives : (e + 1) * negatives], axis=0) for e in range(episodes)]
    for o in range(0, owners, TILE):
        first, second = [dot(one_hot_of_row(h, TILE, float(o)), v) for h, v in zip(hot, value)]
        rows_ref[CAP, o : o + TILE, :] = (first[:, 0:LANES] + second).astype(BF16)
        for s in range(CAP):
            rows_ref[s, o : o + TILE, :] = first[:, (s + 1) * LANES : (s + 2) * LANES].astype(BF16)
    by_owner(rows_ref, flat_ref, wide_ref, CAP + 1, CAP + 1)
    pair_ref[pairs : pairs + 16, :] = numbers_of(pairs_ref, 0)
    numbers_ref[...] = numbers_of(pairs_ref, 1)


def row_numbers(digits):
    digits = digits.astype(F32)
    return digits[0:1, :] * 256.0 + digits[1:2, :]


def vertex_side(pairs_ref, episode, table_ref, theirs_ref):
    column = pairs_ref[0:LANES, 2 * episode : 2 * episode + 1]
    return to_row(column), pair_terms_of(rows_of(column, table_ref), theirs_ref[...].astype(F32))


def context_first(
    flat_ref, pair_ref, numbers_ref, table_ref, pairs_ref,
    send_ref, slots_ref, new_ref, new_state_ref, pair_0_ref, pair_1_ref,
    rows_ref, got_ref, turned_ref, terms_ref, wide_ref, got_wide_ref,
):
    state_ref = pairs_ref.at[LANES + 8 : LANES + 16]
    by_slot(flat_ref, got_ref, got_wide_ref, 0, CAP + 1, CAP + 1)
    slots_ref[...] = got_ref[CAP]
    turn(slots_ref, turned_ref)

    def weigh(s, at, mine):
        there = got_ref[s, pl.ds(at, BLOCK), :].astype(F32)
        terms_ref[s, pl.ds(at, BLOCK), :] = (jax.nn.sigmoid(row_dot(mine, there)) * there).astype(BF16)

    gather_slots(table_ref, slots_ref, rows_ref, 0, 0, 0, weigh)
    n = pair_ref.shape[0] - 16
    row = row_numbers(pair_ref[n : n + 16, :])
    mine = rows_of(to_col(row), table_ref)
    pair_0_ref[...] = mine.astype(BF16)
    pair_terms = pair_terms_of(mine, pair_ref[0:n, :].astype(F32))
    grad_of = scattered(turned_ref, terms_ref, lane_of(0, 0, 0))
    adagrad(table_ref, state_ref, new_ref, new_state_ref, grad_of, row, pair_terms)
    pair_1_ref[...] = rows_of(to_col(row_numbers(numbers_ref[...])), new_ref).astype(BF16)
    gather_slots(new_ref, slots_ref, rows_ref, CAP, 1, 0)
    by_owner(rows_ref, send_ref, wide_ref, 2 * CAP, 2 * CAP)


def vertex_first(
    flat_ref, sent_ref, pairs_ref, partner_ref, table_ref,
    send_ref, pair_ref, new_ref, new_state_ref, turned_ref, rows_ref, terms_ref, wide_ref, got_wide_ref,
):
    state_ref = pairs_ref.at[LANES : LANES + 8]
    turn(sent_ref.at[CAP], turned_ref)
    weigh_flat(sent_ref, 0, flat_ref, got_wide_ref, 2 * CAP, terms_ref)
    row, pair_terms = vertex_side(pairs_ref, 0, table_ref, partner_ref)
    grad_of = scattered(turned_ref, terms_ref, lane_of(0, 0, 2))
    adagrad(table_ref, state_ref, new_ref, new_state_ref, grad_of, row, pair_terms)
    gather_slots(new_ref, sent_ref.at[CAP], rows_ref, 0, 1, 2)
    by_owner(rows_ref, send_ref, wide_ref, CAP, CAP + 1)
    pair_ref[...] = rows_of(pairs_ref[0:LANES, 2:3], new_ref).astype(BF16)


def vertex_last(
    flat_ref, sent_ref, pairs_ref, partner_ref, table_ref, state_ref, slots_ref, context_ref,
    new_ref, new_state_ref, context_rows_ref, context_turned_ref,
    got_ref, rows_ref, turned_ref, terms_ref, got_wide_ref,
):
    gather_slots(context_ref, slots_ref, context_rows_ref, 0, 1, 0)
    turn(slots_ref, context_turned_ref)

    turn(sent_ref.at[CAP], turned_ref)
    by_slot(flat_ref, got_ref, got_wide_ref, CAP, CAP, 2 * CAP)
    gather_slots(table_ref, sent_ref.at[CAP], rows_ref, 0, 1, 2)
    weigh_slots(rows_ref, 0, got_ref, 0, terms_ref)
    row, pair_terms = vertex_side(pairs_ref, 1, table_ref, partner_ref)
    grad_of = scattered(turned_ref, terms_ref, lane_of(1, 0, 2))
    adagrad(table_ref, state_ref, new_ref, new_state_ref, grad_of, row, pair_terms)


def context_last(
    flat_ref, rows_ref, turned_ref, pair_ref, numbers_ref, mine_ref, table_ref, state_ref,
    new_ref, new_state_ref, terms_ref, got_wide_ref,
):
    weigh_flat(rows_ref, 0, flat_ref, got_wide_ref, CAP + 1, terms_ref)
    row = row_numbers(numbers_ref[...])
    pair_terms = pair_terms_of(mine_ref[...].astype(F32), pair_ref[...].astype(F32))
    grad_of = scattered(turned_ref, terms_ref, lane_of(1, 0, 0))
    adagrad(table_ref, state_ref, new_ref, new_state_ref, grad_of, row, pair_terms)


def call(kernel, name, outs, scratch, *args, mib=24):
    return pl.pallas_call(
        kernel,
        name=name,
        out_shape=[jax.ShapeDtypeStruct(s, d) for s, d in outs],
        scratch_shapes=scratch,
        compiler_params=pltpu.CompilerParams(vmem_limit_bytes=mib * 1024 * 1024),
        cost_estimate=pl.CostEstimate(flops=600_000_000, bytes_accessed=4_000_000, transcendentals=2000),
    )(*args)


def exchange(flat, n):
    shape = flat.shape
    per = shape[0] // n
    sub = 2 if per % 4 else 4
    split = flat.reshape(n, per // sub, sub, shape[1]) if per > sub else flat.reshape(n, per, shape[1])
    return lax.all_to_all(split, AXES, split_axis=0, concat_axis=0, tiled=True).reshape(shape)


def passed_along(block, distance, n_devices):
    return lax.ppermute(block, AXES, [((i - distance) % n_devices, i) for i in range(n_devices)])


def body(
    vertex_table, context_table, vertex_state, context_state, pair_blocks, pair_offsets, negative_owner, negative_row
):
    n_type = lax.axis_size("type")
    n = lax.axis_size("dom") * n_type
    rows, width = vertex_table.shape
    episodes, block_pairs, per_block, negatives = negative_owner.shape
    n_pairs = block_pairs * per_block
    shifts = [1 + n_type * (e + 1) for e in range(episodes)]
    owner = negative_owner.transpose(0, 3, 1, 2)
    target = negative_row.transpose(0, 3, 1, 2)
    block = pair_blocks.transpose(0, 2, 1)
    offset = pair_offsets.transpose(0, 1, 3, 2)
    v_state = vertex_state.reshape(rows // TILE, TILE)
    c_state = context_state.reshape(rows // TILE, TILE)

    table = ((rows, width), BF16)
    state = ((rows // TILE, TILE), F32)

    def flat(slots):
        return ((n * slots, width), BF16)

    def slots(number):
        return ((number, n, width), BF16)

    def wide(slots):
        return pltpu.VMEM((n * slots, width), F32)

    turned = pltpu.VMEM((LANES, n), F32)
    terms = pltpu.VMEM((CAP, n, width), BF16)

    pair_rows = ((n_pairs, width), BF16)
    assert n_pairs == LANES
    flat_a, rows_a, pair_a, pairs, numbers = call(
        first_kernel, "slots",
        [flat(CAP + 1), slots(CAP + 1), ((n_pairs + 16, width), BF16), ((n_pairs + 16, LANES), F32), ((16, LANES), BF16)],
        [wide(CAP + 1)], owner, target, block, offset, vertex_table, v_state, c_state, mib=60,
    )
    got_pair_a = passed_along(pair_a, n - shifts[0], n)
    got_numbers = passed_along(numbers, n - shifts[1], n)
    got_a = exchange(flat_a, n)
    flat_b, slots_b, context_1, c_state_1, pair_b0, pair_b1 = call(
        context_first, "context_first",
        [flat(2 * CAP), ((n, LANES), BF16), table, state, pair_rows, pair_rows],
        [pltpu.VMEM((2 * CAP, n, width), BF16), pltpu.VMEM((CAP + 1, n, width), BF16), turned, terms, wide(2 * CAP), wide(CAP + 1)],
        got_a, got_pair_a, got_numbers, context_table, pairs,
    )
    theirs_0 = passed_along(pair_b0, shifts[0], n)
    theirs_1 = passed_along(pair_b1, shifts[1], n)
    got_b = exchange(flat_b, n)
    got_b, theirs_0, theirs_1 = lax.optimization_barrier((got_b, theirs_0, theirs_1))
    flat_c, pair_c, vertex_1, v_state_1 = call(
        vertex_first, "vertex_first", [flat(CAP + 1), pair_rows, table, state],
        [turned, terms, terms, wide(CAP + 1), wide(2 * CAP)],
        got_b, rows_a, pairs, theirs_0, vertex_table,
    )
    got_pair_c = passed_along(pair_c, n - shifts[1], n)
    got_c = exchange(flat_c, n)
    vertex_2, v_state_2, rows_b, turned_b = call(
        vertex_last, "vertex_last", [table, state, slots(CAP), ((LANES, n), F32)],
        [terms, terms, turned, terms, wide(2 * CAP)],
        got_b, rows_a, pairs, theirs_1, vertex_1, v_state_1, slots_b, context_1,
    )
    context_2, c_state_2 = call(
        context_last, "context_last", [table, state], [terms, wide(CAP + 1)],
        got_c, rows_b, turned_b, got_pair_c, got_numbers, pair_b1, context_1, c_state_1,
    )
    return vertex_2, context_2, v_state_2.reshape(rows), c_state_2.reshape(rows)


def solution(mesh):
    in_specs = (
        P(AXES, None),
        P(AXES, None),
        P(AXES),
        P(AXES),
        P(None, AXES, None),
        P(None, AXES, None, None),
        P(None, AXES, None, None),
        P(None, AXES, None, None),
    )
    out_specs = (P(AXES, None), P(AXES, None), P(AXES), P(AXES))
    return jax.shard_map(body, mesh=mesh, in_specs=in_specs, out_specs=out_specs, check_vma=False)
```
